512 devices in a mesh: slab: 16 (over y_lo, z), group: 32 (over x, y_hi, core).
Axes of the slice: x: 4, y: 8 (y_hi: 4, y_lo: 2; y = y_hi * 2 + y_lo), z: 8, core: 2. Of those that a mesh axis runs over, the one named last changes fastest.
Arguments:
- images: bfloat16 [131072, 768], P(('slab', 'group')), may hold values from -200 to 200
- references: bfloat16 [8192, 768], P(('slab', 'group')), may hold values from -4 to 4
- ctf_table: float32 [32, 384], replicated, may hold values from -1.3 to 1.3
- ctf_ids: int32 [131072], P(('slab', 'group')), may hold values from 0 to 31
- owners: int32 [131072], P(('slab', 'group')), may hold values from 0 to 15, as said below
Outputs:
- new_references: float32 [8192, 768], P(('slab', 'group'))
- log_evidence: float32 [131072], P(('slab', 'group'))
The draws below stay inside these ranges and needn't reach their ends.
Inputs may be any that keep to these rules, and one draw needn't show every extreme that they name: `owners`: no slab is named by more than 48 lines of one device's 256, and in every device's lines one slab is named by exactly 48.
All inputs are finite; a program needn't handle non-finite values.
Results may differ from the reference program's by a relative error of at most 0.003.
Values may be sent and summed in bfloat16 or wider, within the bound.
A program may use at most 64 MiB of HBM per device.

```python
import math
import jax
import jax.numpy as jnp
from jax import lax

L = 384
LW = 768
K_LOC = 512
ROWS_DEV = 256
CTF_GROUPS = 32
CAP = 48
K_TOT = 8192
ROWS_TOT = 131072
N_SLAB = 16


def route_block(block_key):
    sub_keys = jax.random.split(block_key, 4)
    hottest = jax.random.randint(sub_keys[0], (), 0, N_SLAB)
    second = (hottest + jax.random.randint(sub_keys[1], (), 1, N_SLAB)) % N_SLAB
    upper = min(CAP, ROWS_DEV - CAP)
    second_count = jax.random.randint(sub_keys[2], (), upper // 2, upper + 1)
    position = jnp.arange(ROWS_DEV, dtype=jnp.int32)
    others = (position - CAP - second_count) % (N_SLAB - 2)
    lesser = jnp.minimum(hottest, second)
    greater = jnp.maximum(hottest, second)
    others = others + (others >= lesser).astype(jnp.int32)
    others = others + (others >= greater).astype(jnp.int32)
    labels = jnp.where(position < CAP, hottest, jnp.where(position < CAP + second_count, second, others))
    return labels[jax.random.permutation(sub_keys[3], ROWS_DEV)]


def route_table(key):
    block_keys = jax.random.split(jax.random.fold_in(key, 21), ROWS_TOT // ROWS_DEV)
    return jax.vmap(route_block)(block_keys).reshape(ROWS_TOT).astype(jnp.int32)


def group_table(key):
    return jax.random.randint(jax.random.fold_in(key, 31), (ROWS_TOT,), 0, CTF_GROUPS).astype(jnp.int32)


def ctf_values(key):
    sub_keys = jax.random.split(jax.random.fold_in(key, 41), 2)
    defocus = jnp.exp(jax.random.uniform(sub_keys[0], (CTF_GROUPS, 1), jnp.float32, 0.0, math.log(3.0)))
    frequency = jnp.arange(L, dtype=jnp.float32) / L
    phase = 2.0 * math.pi * 6.0 * defocus * frequency[None, :] ** 2 + 0.3
    envelope = jnp.exp(-1.5 * frequency * frequency)
    rough = jax.random.uniform(sub_keys[1], (CTF_GROUPS, L), jnp.float32, 0.7, 1.3)
    return -envelope[None, :] * jnp.sin(phase) * rough


def ref_values(key):
    sub_keys = jax.random.split(jax.random.fold_in(key, 51), 2)
    return jax.random.truncated_normal(sub_keys[1], -4.0, 4.0, (K_TOT, LW), jnp.float32)


def draw_images(key, part):
    sub_keys = jax.random.split(jax.random.fold_in(key, 61), 2)
    return jax.random.truncated_normal(sub_keys[1], -5.0, 5.0, (ROWS_TOT, LW), jnp.float32).astype(jnp.bfloat16)


def draw_references(key, part):
    return ref_values(key).astype(jnp.bfloat16)


def draw_ctf_table(key, part):
    return ctf_values(key)


def draw_ctf_ids(key, part):
    return group_table(key)


def draw_owners(key, part):
    return route_table(key)


def setup_inputs(seed: int = 0) -> dict:
    arg_keys = jax.random.split(jax.random.key(seed), 6)
    images = draw_images(jax.random.fold_in(arg_keys[5], 71), 0)
    references = draw_references(jax.random.fold_in(arg_keys[5], 71), 0)
    ctf_table = draw_ctf_table(jax.random.fold_in(arg_keys[5], 71), 0)
    ctf_ids = draw_ctf_ids(jax.random.fold_in(arg_keys[5], 71), 0)
    owners = draw_owners(jax.random.fold_in(arg_keys[5], 71), 0)
    return dict(images=images, references=references, ctf_table=ctf_table, ctf_ids=ctf_ids, owners=owners)


def slot_plan(owner_block, slab_count, capacity):
    line_count = owner_block.shape[0]
    one_hot = (owner_block[:, None] == jnp.arange(slab_count, dtype=jnp.int32)[None, :]).astype(jnp.int32)
    earlier = jnp.cumsum(one_hot, axis=0) - one_hot
    rank_index = jnp.sum(earlier * one_hot, axis=1)
    slot_index = (owner_block * capacity + rank_index).astype(jnp.int32)
    filled_slot = jnp.zeros((slab_count * capacity,), jnp.int32).at[slot_index].set(jnp.arange(line_count, dtype=jnp.int32) + 1)
    filled_mask = filled_slot > 0
    source_row = jnp.maximum(filled_slot - 1, 0).astype(jnp.int32)
    return slot_index, source_row, filled_mask


def weigh(image_slots, ctf_tags, ctf_table):
    group_count = ctf_table.shape[0]
    levels = jnp.arange(1, group_count + 1, dtype=jnp.float32)
    group_pick = (ctf_tags.astype(jnp.float32)[:, None] == levels[None, :]).astype(jnp.float32)
    ctf_rows = jnp.dot(group_pick, ctf_table, precision=lax.Precision.HIGHEST)
    weighted = (image_slots.astype(jnp.float32) * jnp.concatenate([ctf_rows, ctf_rows], axis=1)).astype(jnp.bfloat16)
    ctf_square = (ctf_rows * ctf_rows).astype(jnp.bfloat16)
    return weighted, ctf_square


def score_block(weighted, ctf_square, ref_lines):
    half_width = ref_lines.shape[1] // 2
    widened = ref_lines.astype(jnp.float32)
    line_power = (widened[:, :half_width] ** 2 + widened[:, half_width:] ** 2).astype(jnp.bfloat16)
    cross_term = lax.dot_general(weighted, ref_lines, (((1,), (1,)), ((), ())), preferred_element_type=jnp.float32)
    quad_term = lax.dot_general(ctf_square, line_power, (((1,), (1,)), ((), ())), preferred_element_type=jnp.float32)
    return (cross_term - 0.5 * quad_term) * (ref_lines.shape[1] ** -0.5)


def finish(scores, filled_mask):
    score_max = jnp.max(scores, axis=1, keepdims=True)
    exp_total = jnp.sum(jnp.exp(scores - score_max), axis=1, keepdims=True)
    evidence = score_max + jnp.log(exp_total)
    responsibility = (jnp.exp(scores - evidence) * filled_mask[:, None].astype(jnp.float32)).astype(jnp.bfloat16)
    return responsibility, evidence[:, 0]


def accumulate(responsibility, weighted, ctf_square):
    numerator = lax.dot_general(responsibility, weighted, (((0,), (0,)), ((), ())), preferred_element_type=jnp.float32)
    denominator = lax.dot_general(responsibility, ctf_square, (((0,), (0,)), ((), ())), preferred_element_type=jnp.float32)
    return numerator, denominator


def reference(images, references, ctf_table, ctf_ids, owners):
    block_count = ROWS_TOT // ROWS_DEV
    ref_slabs = references.reshape(N_SLAB, K_LOC, LW)

    def one_block(running, block_inputs):
        image_block, group_block, owner_block = block_inputs
        slot_index, source_row, filled_mask = slot_plan(owner_block, N_SLAB, CAP)
        image_slots = jnp.where(filled_mask[:, None], image_block[source_row], jnp.zeros((), jnp.bfloat16))
        ctf_tags = jnp.where(filled_mask, group_block[source_row] + 1, 0).astype(jnp.float32)
        weighted, ctf_square = weigh(image_slots, ctf_tags, ctf_table)
        weighted = weighted.reshape(N_SLAB, CAP, LW)
        ctf_square = ctf_square.reshape(N_SLAB, CAP, L)
        scores = jax.vmap(score_block)(weighted, ctf_square, ref_slabs)
        responsibility, evidence = jax.vmap(finish)(scores, filled_mask.reshape(N_SLAB, CAP))
        numerator, denominator = jax.vmap(accumulate)(responsibility, weighted, ctf_square)
        line_evidence = evidence.reshape(N_SLAB * CAP)[slot_index]
        return (running[0] + numerator, running[1] + denominator), line_evidence

    start_sums = (jnp.zeros((N_SLAB, K_LOC, LW), jnp.float32), jnp.zeros((N_SLAB, K_LOC, L), jnp.float32))
    sums, evidence_rows = lax.scan(one_block, start_sums, (images.reshape(block_count, ROWS_DEV, LW), ctf_ids.reshape(block_count, ROWS_DEV), owners.reshape(block_count, ROWS_DEV)))
    numerator, denominator = sums
    new_references = numerator / (jnp.concatenate([denominator, denominator], axis=2) + 1.0)
    return new_references.reshape(K_TOT, LW), evidence_rows.reshape(ROWS_TOT)
```

```python
import functools

import jax
import jax.numpy as jnp
from jax import lax
from jax.experimental import pallas as pl
from jax.experimental.pallas import tpu as pltpu
from jax.sharding import PartitionSpec as P

F32, BF16 = jnp.float32, jnp.bfloat16
MESH = pl.DeviceIdType.MESH
N_YLO, N_Z = 2, 8
N_X, N_YHI, N_CORE = 4, 4, 2
OFFSETS = (
    (0, 0), (1, 0), (0, 1), (1, 1),
    (0, 7), (1, 7), (0, 2), (1, 2),
    (0, 6), (1, 6), (0, 3), (1, 3),
    (0, 5), (1, 5), (0, 4), (1, 4),
)
PER_BATCH = 4


def nt(a, b):
    return lax.dot_general(a, b, (((1,), (1,)), ((), ())), preferred_element_type=F32)


def tn(a, b):
    return lax.dot_general(a, b, (((0,), (0,)), ((), ())), preferred_element_type=F32)


def nn(a, b):
    return jnp.dot(a, b, preferred_element_type=F32)


def three(v):
    hi = v.astype(BF16)
    rest = v - hi.astype(F32)
    mid = rest.astype(BF16)
    return hi, mid, (rest - mid.astype(F32)).astype(BF16)


def iota(shape, dim):
    return lax.broadcasted_iota(jnp.int32, shape, dim)


def kernel(
    img, refs, ctf, ids, own,
    out, line_ev,
    weighted, send_lines, lines, send_tags, tags, send_ev, ev,
    ref_all, resp, quad, acc, racc, own_rows,
    core_in, rcore_out, rcore_in, x_out, x_in, rx_out, rx_in, y_out, y_in, ry_out, ry_in,
    s_line, r_line, s_tag, r_tag, s_ev, r_ev,
    s_agy, r_agy, s_agx, r_agx, s_agc, r_agc,
    s_rsc, r_rsc, s_rcc, r_rcc, s_rsx, r_rsx, s_rcx, r_rcx, s_rsy, r_rsy, s_rcy, r_rcy,
):
    rows, width = img.shape
    half = width // 2
    groups = ctf.shape[0]
    n = N_YLO * N_Z
    cap = 3 * rows // n
    batches = n // PER_BATCH
    span = PER_BATCH * cap
    slab, group = lax.axis_index("slab"), lax.axis_index("group")
    y_lo, z = slab // N_Z, slab % N_Z
    x, y_hi, core = group // (N_YHI * N_CORE), (group // N_CORE) % N_YHI, group % N_CORE

    def slab_at(dy, dz):
        return ((y_lo + dy + N_YLO) % N_YLO) * N_Z + (z + dz + N_Z) % N_Z

    def to(k):
        return (slab_at(*OFFSETS[k]), group)

    def back(k):
        return (slab_at(-OFFSETS[k][0], -OFFSETS[k][1]), group)

    def x_peer(d):
        return (slab, (((x + d) % N_X) * N_YHI + y_hi) * N_CORE + core)

    def y_peer(d):
        return (slab, (x * N_YHI + (y_hi + d) % N_YHI) * N_CORE + core)

    sibling = (slab, group + 1 - 2 * core)

    def copy(src, dst, send, recv, device):
        return pltpu.make_async_remote_copy(
            src_ref=src, dst_ref=dst, send_sem=send, recv_sem=recv, device_id=device, device_id_type=MESH
        )

    barrier = pltpu.get_barrier_semaphore()
    partners = [to(k) for k in range(1, n)]
    partners += [x_peer(d) for d in range(1, N_X)] + [y_peer(d) for d in range(1, N_YHI)] + [sibling]
    for p in partners:
        pl.semaphore_signal(barrier, inc=1, device_id=p, device_id_type=MESH)

    target = iota((n, rows), 0)
    wanted = jnp.zeros((n, rows), jnp.int32)
    for k in range(n):
        wanted = jnp.where(target == k, slab_at(*OFFSETS[k]), wanted)
    hot = (wanted == own[...]).astype(F32)
    hot_b = hot.astype(BF16)
    before = (iota((rows, rows), 0) < iota((rows, rows), 1)).astype(F32).astype(BF16)
    rank = jnp.sum(hot * nn(hot_b, before), axis=0, keepdims=True)
    line_k = jnp.sum(hot * target.astype(F32), axis=0, keepdims=True)
    slot = (line_k * cap + rank).astype(jnp.int32)
    tag_row = (ids[...] + 1).astype(F32)
    rank_hot = (iota((128, rows), 0) == rank.astype(jnp.int32)).astype(F32).astype(BF16)
    tag_slots = nt((hot * tag_row).astype(BF16), rank_hot)
    for k in range(n):
        send_tags[k] = jnp.broadcast_to(tag_slots[k : k + 1, :], (8, 128))

    pick = (iota((groups, rows), 0) == ids[...]).astype(F32).astype(BF16)
    ctf_hi, ctf_mid, ctf_lo = three(ctf[...])
    ctf_rows = tn(pick, ctf_hi) + tn(pick, ctf_mid) + tn(pick, ctf_lo)
    weighted[:, :half] = (img[:, :half].astype(F32) * ctf_rows).astype(BF16)
    weighted[:, half:] = (img[:, half:].astype(F32) * ctf_rows).astype(BF16)

    pl.semaphore_wait(barrier, len(partners))

    ref_all[core, x, y_hi] = refs[...]
    ag_y = [copy(refs, ref_all.at[core, x, y_hi], s_agy.at[d - 1], r_agy.at[d - 1], y_peer(d)) for d in range(1, N_YHI)]
    for c in ag_y:
        c.start()

    sends = []
    for b in reversed(range(batches)):
        place = (iota((span, rows), 0) + b * span == slot).astype(F32).astype(BF16)
        packed = nn(place, weighted[...]).astype(BF16)
        for j in reversed(range(PER_BATCH)):
            k = b * PER_BATCH + j
            part = packed[j * cap : (j + 1) * cap]
            if k == 0:
                lines[0] = part
                tags[0] = send_tags[0]
                continue
            send_lines[k] = part
            line_copy = copy(send_lines.at[k], lines.at[k], s_line.at[k], r_line.at[k], to(k))
            tag_copy = copy(send_tags.at[k], tags.at[k], s_tag.at[k], r_tag.at[k], to(k))
            tag_copy.start()
            line_copy.start()
            sends += [tag_copy, line_copy]

    for c in ag_y:
        c.wait_recv()
    mine = ref_all.at[core, x]
    ag_x = [copy(mine, mine, s_agx.at[d - 1], r_agx.at[d - 1], x_peer(d)) for d in range(1, N_X)]
    for c in ag_x:
        c.start()
    ag_c = []
    for d in range(N_X):
        if d:
            ag_x[d - 1].wait_recv()
        piece = ref_all.at[core, (x - d + N_X) % N_X]
        ag_c.append(copy(piece, piece, s_agc.at[d], r_agc.at[d], sibling))
        ag_c[-1].start()
    for c in ag_c:
        c.wait_recv()
    sends += ag_y + ag_x + ag_c

    k_loc = N_CORE * N_X * N_YHI * refs.shape[0]
    row_group = iota((128, half), 0)
    ctf_sq = ctf[...] * ctf[...]
    ctf_sq4 = jnp.concatenate([ctf_sq] * (128 // groups), axis=0).astype(BF16)
    del row_group
    reference = ref_all[...].reshape(k_loc, width)
    re, im = reference[:, :half].astype(F32), reference[:, half:].astype(F32)
    power = (re * re + im * im).astype(BF16)
    hi, mid, lo = three(-0.5 * nt(power, ctf_sq4))
    lane = iota((k_loc, 128), 1)
    zero = jnp.zeros((k_loc, 128), F32)
    quad[...] = jnp.where(
        lane < groups, hi.astype(F32),
        jnp.where(lane < 2 * groups, mid.astype(F32), jnp.where(lane < 3 * groups, lo.astype(F32), zero)),
    ).astype(BF16)

    scale = width**-0.5
    spread = (iota((128, span), 0) == iota((128, span), 1) % cap).astype(F32).astype(BF16)
    mine_8 = (iota((PER_BATCH * 8, span), 0) == 8 * (iota((PER_BATCH * 8, span), 1) // cap)).astype(F32)
    tag_of = (iota((128, span), 0) % groups + 1).astype(F32)
    h_rows = k_loc // N_CORE
    ev_sends, core_sends = [], []
    for b in range(batches):
        for j in range(PER_BATCH):
            k = b * PER_BATCH + j
            if k:
                copy(send_tags.at[k], tags.at[k], s_tag.at[k], r_tag.at[k], to(k)).wait_recv()
                copy(send_lines.at[k], lines.at[k], s_line.at[k], r_line.at[k], to(k)).wait_recv()
        batch = lines[b * PER_BATCH : (b + 1) * PER_BATCH].reshape(span, width)
        tag8 = tags[b * PER_BATCH : (b + 1) * PER_BATCH].reshape(PER_BATCH * 8, 128).astype(BF16)
        tag = jnp.sum(nn(tag8, spread) * mine_8, axis=0, keepdims=True)
        chosen = (tag_of == tag).astype(F32).astype(BF16)
        score = (nt(ref_all[...].reshape(k_loc, width), batch) + nn(quad[...], chosen)) * scale
        top = jnp.max(score, axis=0, keepdims=True)
        e = jnp.exp(score - top)
        total = jnp.sum(e, axis=0, keepdims=True)
        resp[...] = (e * (1.0 / total)).astype(BF16)
        evidence = top + jnp.log(total)
        send_ev[b, :, :span] = jnp.broadcast_to(evidence, (8, span))
        send_ev[b, :, span:] = jnp.zeros((8, 256 - span), F32)
        for j in range(PER_BATCH):
            k = b * PER_BATCH + j
            if k:
                ev_copy = copy(send_ev.at[b], ev.at[k], s_ev.at[k], r_ev.at[k], back(k))
                ev_copy.start()
                ev_sends.append(ev_copy)
            else:
                ev[0] = send_ev[0]
        for other in (1, 0):
            c = (core + other) % N_CORE
            r = resp[pl.ds(pl.multiple_of(c * h_rows, h_rows), h_rows), :]
            num = nn(r, batch)
            cnt = nt(r, chosen)
            if b:
                num += acc[c]
                cnt += racc[c]
            acc[c] = num
            racc[c] = cnt
            if b == batches - 1 and other:
                fold = jnp.where(iota((h_rows, 128), 1) // groups == (iota((h_rows, 128), 0) // refs.shape[0]) % N_YHI, cnt, 0.0)
                rcore_out[...] = jnp.sum(fold.reshape(N_X, N_YHI, refs.shape[0], 128), axis=1)
                rc = copy(rcore_out, rcore_in, s_rcc, r_rcc, sibling)
                rc.start()
                core_sends.append(rc)
                x_rows = h_rows // N_X
                for i, d in enumerate((2, 1, 3, 0)):
                    at = pl.ds(pl.multiple_of(((x + d) % N_X) * x_rows, x_rows), x_rows)
                    cc = copy(acc.at[c, at], core_in.at[at], s_rsc.at[i], r_rsc.at[i], sibling)
                    cc.start()
                    core_sends.append(cc)

    cnt = racc[core]
    fold = jnp.where(iota((h_rows, 128), 1) // groups == (iota((h_rows, 128), 0) // refs.shape[0]) % N_YHI, cnt, 0.0)
    fold = jnp.sum(fold.reshape(N_X, N_YHI, refs.shape[0], 128), axis=1)
    core_sends[0].wait_recv()
    rx_out[...] = fold + rcore_in[...]
    x_sends = []
    for i, d in enumerate((2, 1, 3, 0)):
        xp = (x + d) % N_X
        at = pl.ds(pl.multiple_of(xp * x_rows, x_rows), x_rows)
        core_sends[1 + i].wait_recv()
        both = acc[core, at] + core_in[at]
        if d == 0:
            own_sum = both
            continue
        x_out[d - 1] = both.astype(BF16)
        xc = copy(x_out.at[d - 1], x_in.at[d - 1], s_rsx.at[d - 1], r_rsx.at[d - 1], x_peer(d))
        rc = copy(rx_out.at[xp], rx_in.at[d - 1], s_rcx.at[d - 1], r_rcx.at[d - 1], x_peer(d))
        rc.start()
        xc.start()
        x_sends += [rc, xc]
    own_cnt = rx_out[x]
    for c in x_sends:
        c.wait_recv()
    for d in range(1, N_X):
        own_sum += x_in[d - 1].astype(F32)
        own_cnt += rx_in[d - 1]

    ry_out[...] = own_cnt
    own_rows[...] = own_sum
    y_sends = []
    for d in (2, 1, 3):
        at = pl.ds(pl.multiple_of(((y_hi + d) % N_YHI) * refs.shape[0], refs.shape[0]), refs.shape[0])
        y_out[d - 1] = own_rows[at].astype(BF16)
        yc = copy(y_out.at[d - 1], y_in.at[d - 1], s_rsy.at[d - 1], r_rsy.at[d - 1], y_peer(d))
        rc = copy(ry_out, ry_in.at[d - 1], s_rcy.at[d - 1], r_rcy.at[d - 1], y_peer(d))
        rc.start()
        yc.start()
        y_sends += [rc, yc]

    for c in ev_sends:
        c.wait_recv()
    at_lane = line_k - PER_BATCH * jnp.floor(line_k * (1.0 / PER_BATCH))
    lane_hot = (iota((256, rows), 0) == (at_lane * cap + rank).astype(jnp.int32)).astype(F32).astype(BF16)
    e_hi, e_mid, e_lo = three(ev[:, 0, :])
    by_target = nn(e_hi, lane_hot) + nn(e_mid, lane_hot) + nn(e_lo, lane_hot)
    line_ev[...] = jnp.sum(hot * by_target, axis=0, keepdims=True)

    final = own_rows[pl.ds(pl.multiple_of(y_hi * refs.shape[0], refs.shape[0]), refs.shape[0])]
    cnt = own_cnt
    for c in y_sends:
        c.wait_recv()
    for d in range(1, N_YHI):
        final += y_in[d - 1].astype(F32)
        cnt += ry_in[d - 1]
    cnt = jnp.where(iota(cnt.shape, 1) // groups == y_hi, cnt, 0.0)
    c_hi, c_mid, c_lo = three(cnt)
    den = nn(c_hi, ctf_sq4) + nn(c_mid, ctf_sq4) + nn(c_lo, ctf_sq4) + 1.0
    out[:, :half] = final[:, :half] / den
    out[:, half:] = final[:, half:] / den

    for c in sends + ev_sends + core_sends + x_sends + y_sends:
        c.wait_send()


def on_device(images, references, ctf_table, ctf_ids, owners):
    rows, width = images.shape
    per = references.shape[0]
    n = N_YLO * N_Z
    cap = 3 * rows // n
    h_rows = N_X * N_YHI * per
    x_rows = N_YHI * per
    dma = pltpu.SemaphoreType.DMA
    vm = pltpu.VMEM
    scratch = [
        vm((rows, width), BF16), vm((n, cap, width), BF16), vm((n, cap, width), BF16),
        vm((n, 8, 128), F32), vm((n, 8, 128), F32), vm((n // PER_BATCH, 8, 256), F32), vm((n, 8, 256), F32),
        vm((N_CORE, N_X, N_YHI, per, width), BF16), vm((N_CORE * h_rows, PER_BATCH * cap), BF16),
        vm((N_CORE * h_rows, 128), BF16), vm((N_CORE, h_rows, width), F32), vm((N_CORE, h_rows, 128), F32), vm((x_rows, width), F32),
        vm((h_rows, width), F32), vm((N_X, per, 128), F32), vm((N_X, per, 128), F32),
        vm((N_X - 1, x_rows, width), BF16), vm((N_X - 1, x_rows, width), BF16),
        vm((N_X, per, 128), F32), vm((N_X - 1, per, 128), F32),
        vm((N_YHI - 1, per, width), BF16), vm((N_YHI - 1, per, width), BF16),
        vm((per, 128), F32), vm((N_YHI - 1, per, 128), F32),
        *[dma((n,))] * 6,
        *[dma((N_YHI - 1,))] * 2, *[dma((N_X - 1,))] * 2, *[dma((N_X,))] * 2,
        *[dma((N_X,))] * 2, dma, dma, *[dma((N_X - 1,))] * 4, *[dma((N_YHI - 1,))] * 4,
    ]
    new, ev = pl.pallas_call(
        kernel,
        out_shape=(jax.ShapeDtypeStruct((per, width), F32), jax.ShapeDtypeStruct((1, rows), F32)),
        in_specs=[pl.BlockSpec(memory_space=pltpu.VMEM)] * 5,
        out_specs=[pl.BlockSpec(memory_space=pltpu.VMEM)] * 2,
        scratch_shapes=scratch,
        compiler_params=pltpu.CompilerParams(
            collective_id=0, has_side_effects=True, vmem_limit_bytes=48 * 2**20
        ),
    )(images, references, ctf_table, ctf_ids.reshape(1, rows), owners.reshape(1, rows))
    return new, ev.reshape(rows)


def solution(mesh):
    both = P(("slab", "group"))
    rows = P(("slab", "group"), None)
    return jax.shard_map(
        on_device, mesh=mesh, in_specs=(rows, rows, P(), both, both), out_specs=(rows, both), check_vma=False
    )
```

```python
import functools

import jax
import jax.numpy as jnp
from jax import lax
from jax.experimental import pallas as pl
from jax.experimental.pallas import tpu as pltpu
from jax.sharding import PartitionSpec as P

F32, BF16 = jnp.float32, jnp.bfloat16
MESH = pl.DeviceIdType.MESH
N_X, N_Y, N_Z = 4, 8, 8
N_YLO, N_YHI, N_CORE = 2, 4, 2
FAR = N_Z // 2
OFFSETS = tuple((dz, dx * (1 - 2 * dy), dy) for dz in (0, 1, -1, 2) for dy in (0, 1) for dx in (0, 1))
PER_BATCH = 4


def nt(a, b):
    return lax.dot_general(a, b, (((1,), (1,)), ((), ())), preferred_element_type=F32)


def tn(a, b):
    return lax.dot_general(a, b, (((0,), (0,)), ((), ())), preferred_element_type=F32)


def nn(a, b):
    return jnp.dot(a, b, preferred_element_type=F32)


def three(v):
    hi = v.astype(BF16)
    rest = v - hi.astype(F32)
    mid = rest.astype(BF16)
    return hi, mid, (rest - mid.astype(F32)).astype(BF16)


def iota(shape, dim):
    return lax.broadcasted_iota(jnp.int32, shape, dim)


def kernel(
    img, refs, ctf, ids, own,
    out, line_ev,
    weighted, send_lines, lines, send_tags, tags, send_ev, ev,
    ref_all, resp, quad, acc, racc,
    core_in, rcore_out, rcore_in, x_out, x_in, rx_out, rx_in, own_rows, y_out, y_in, ry_out, ry_in,
    fin_out, fin_in,
    s_line, r_line, s_tag, r_tag, s_ev, r_ev,
    s_ag, r_ag, s_agy, r_agy, s_agx, r_agx, s_agc, r_agc,
    s_rsc, r_rsc, s_rcc, r_rcc, s_rsx, r_rsx, s_rcx, r_rcx, s_rsy, r_rsy, s_rcy, r_rcy,
    s_fin, r_fin,
):
    rows, width = img.shape
    per = refs.shape[0]
    half = width // 2
    groups = ctf.shape[0]
    n = len(OFFSETS)
    cap = 3 * rows // n
    batches = n // PER_BATCH
    span = PER_BATCH * cap
    slab, group = lax.axis_index("slab"), lax.axis_index("group")
    y_lo, z = slab // N_Z, slab % N_Z
    x, y_hi, core = group // (N_YHI * N_CORE), (group // N_CORE) % N_YHI, group % N_CORE
    y = N_YLO * y_hi + y_lo
    way = 1 - 2 * core
    odd, pair = x % 2, x // 2

    def device(dz, dx, dy):
        x_to, y_to, z_to = (x + dx + N_X) % N_X, (y + dy + N_Y) % N_Y, (z + dz + N_Z) % N_Z
        return (y_to % N_YLO) * N_Z + z_to, (x_to * N_YHI + y_to // N_YLO) * N_CORE + core

    def to(k):
        return device(*(way * d for d in OFFSETS[k]))

    def back(k):
        return device(*(-way * d for d in OFFSETS[k]))

    def slab_of(k):
        dz, dx, dy = (way * d for d in OFFSETS[k])
        return ((y + dy + N_Y) % N_YLO) * N_Z + (z + dz + N_Z + FAR * ((x + dx + N_X) % 2)) % N_Z

    def y_peer(d):
        return device(0, 0, N_YLO * d)

    x_peer = device(0, 2, 0)
    sibling = (slab, group + way)
    near, across, beyond = device(0, 1 - 2 * odd, 0), device(FAR, 1 - 2 * odd, 0), device(FAR, 0, 0)

    def choose(a, b):
        return tuple(odd * v + (1 - odd) * u for u, v in zip(a, b))

    def copy(src, dst, send, recv, device):
        return pltpu.make_async_remote_copy(
            src_ref=src, dst_ref=dst, send_sem=send, recv_sem=recv, device_id=device, device_id_type=MESH
        )

    barrier = pltpu.get_barrier_semaphore()
    partners = [to(k) for k in range(1, n)] + [back(k) for k in range(1, n)]
    partners += [y_peer(d) for d in range(1, N_YHI)] + [x_peer, sibling, near, across]
    for p in partners:
        pl.semaphore_signal(barrier, inc=1, device_id=p, device_id_type=MESH)

    @pl.when(odd == 1)
    def _():
        pl.semaphore_signal(barrier, inc=1, device_id=beyond, device_id_type=MESH)

    target = iota((n, rows), 0)
    wanted = jnp.zeros((n, rows), jnp.int32)
    for k in range(n):
        wanted = jnp.where(target == k, slab_of(k), wanted)
    hot = (wanted == own[...]).astype(F32)
    hot_b = hot.astype(BF16)
    before = (iota((rows, rows), 0) < iota((rows, rows), 1)).astype(F32).astype(BF16)
    rank = jnp.sum(hot * nn(hot_b, before), axis=0, keepdims=True)
    line_k = jnp.sum(hot * target.astype(F32), axis=0, keepdims=True)
    slot = (line_k * cap + rank).astype(jnp.int32)
    tag_row = (ids[...] + 1).astype(F32)
    rank_hot = (iota((128, rows), 0) == rank.astype(jnp.int32)).astype(F32).astype(BF16)
    tag_slots = nt((hot * tag_row).astype(BF16), rank_hot)
    for k in range(n):
        send_tags[k] = jnp.broadcast_to(tag_slots[k : k + 1, :], (8, 128))

    pick = (iota((groups, rows), 0) == ids[...]).astype(F32).astype(BF16)
    ctf_hi, ctf_mid, ctf_lo = three(ctf[...])
    ctf_rows = tn(pick, ctf_hi) + tn(pick, ctf_mid) + tn(pick, ctf_lo)
    weighted[:, :half] = (img[:, :half].astype(F32) * ctf_rows).astype(BF16)
    weighted[:, half:] = (img[:, half:].astype(F32) * ctf_rows).astype(BF16)

    pl.semaphore_wait(barrier, len(partners) + odd)

    slot_ref = ref_all.at[core, pair, y_hi, odd]
    ag = copy(refs, slot_ref, s_ag.at[0], r_ag.at[odd], choose(across, near))
    ag.start()
    ag_2 = copy(refs, slot_ref, s_ag.at[1], r_ag.at[1], beyond)

    @pl.when(odd == 1)
    def _():
        ag_2.start()

    @pl.when(odd == 0)
    def _():
        ref_all[core, pair, y_hi, 0] = refs[...]

    sends = []
    for b in reversed(range(batches)):
        place = (iota((span, rows), 0) + b * span == slot).astype(F32).astype(BF16)
        packed = nn(place, weighted[...]).astype(BF16)
        for j in reversed(range(PER_BATCH)):
            k = b * PER_BATCH + j
            part = packed[j * cap : (j + 1) * cap]
            if k == 0:
                lines[0] = part
                tags[0] = send_tags[0]
                continue
            send_lines[k] = part
            line_copy = copy(send_lines.at[k], lines.at[k], s_line.at[k], r_line.at[k], to(k))
            tag_copy = copy(send_tags.at[k], tags.at[k], s_tag.at[k], r_tag.at[k], to(k))
            tag_copy.start()
            line_copy.start()
            sends += [tag_copy, line_copy]

    @pl.when(odd == 1)
    def _():
        copy(refs, ref_all.at[core, pair, y_hi, 0], s_ag.at[0], r_ag.at[0], across).wait_recv()
        ag_2.wait_send()

    copy(refs, ref_all.at[core, pair, y_hi, 1], s_ag.at[0], r_ag.at[1], across).wait_recv()
    mine = ref_all.at[core, pair, y_hi]
    ag_y = [copy(mine, mine, s_agy.at[d - 1], r_agy.at[d - 1], y_peer(d)) for d in range(1, N_YHI)]
    for c in ag_y:
        c.start()
    for c in ag_y:
        c.wait_recv()
    mine, theirs = ref_all.at[core, pair], ref_all.at[core, 1 - pair]
    ag_x = [copy(mine, mine, s_agx, r_agx, x_peer)]
    ag_x[0].start()
    ag_c = [copy(p, p, s_agc.at[i], r_agc.at[i], sibling) for i, p in enumerate((mine, theirs))]
    ag_c[0].start()
    ag_x[0].wait_recv()
    ag_c[1].start()
    for c in ag_c:
        c.wait_recv()
    sends += [ag] + ag_y + ag_x + ag_c

    k_loc = N_CORE * N_X * N_YHI * per
    ctf_sq = ctf[...] * ctf[...]
    ctf_sq4 = jnp.concatenate([ctf_sq] * (128 // groups), axis=0).astype(BF16)
    reference = ref_all[...].reshape(k_loc, width)
    re, im = reference[:, :half].astype(F32), reference[:, half:].astype(F32)
    power = (re * re + im * im).astype(BF16)
    hi, mid, lo = three(-0.5 * nt(power, ctf_sq4))
    lane = iota((k_loc, 128), 1)
    zero = jnp.zeros((k_loc, 128), F32)
    quad[...] = jnp.where(
        lane < groups, hi.astype(F32),
        jnp.where(lane < 2 * groups, mid.astype(F32), jnp.where(lane < 3 * groups, lo.astype(F32), zero)),
    ).astype(BF16)

    scale = width**-0.5
    spread = (iota((128, span), 0) == iota((128, span), 1) % cap).astype(F32).astype(BF16)
    mine_8 = (iota((PER_BATCH * 8, span), 0) == 8 * (iota((PER_BATCH * 8, span), 1) // cap)).astype(F32)
    tag_of = (iota((128, span), 0) % groups + 1).astype(F32)
    h_rows = k_loc // N_CORE
    ev_sends, core_sends = [], []
    for b in range(batches):
        for j in range(PER_BATCH):
            k = b * PER_BATCH + j
            if k:
                copy(send_tags.at[k], tags.at[k], s_tag.at[k], r_tag.at[k], to(k)).wait_recv()
                copy(send_lines.at[k], lines.at[k], s_line.at[k], r_line.at[k], to(k)).wait_recv()
        batch = lines[b * PER_BATCH : (b + 1) * PER_BATCH].reshape(span, width)
        tag8 = tags[b * PER_BATCH : (b + 1) * PER_BATCH].reshape(PER_BATCH * 8, 128).astype(BF16)
        tag = jnp.sum(nn(tag8, spread) * mine_8, axis=0, keepdims=True)
        chosen = (tag_of == tag).astype(F32).astype(BF16)
        score = (nt(ref_all[...].reshape(k_loc, width), batch) + nn(quad[...], chosen)) * scale
        top = jnp.max(score, axis=0, keepdims=True)
        e = jnp.exp(score - top)
        total = jnp.sum(e, axis=0, keepdims=True)
        resp[...] = (e * (1.0 / total)).astype(BF16)
        evidence = top + jnp.log(total)
        send_ev[b, :, :span] = jnp.broadcast_to(evidence, (8, span))
        send_ev[b, :, span:] = jnp.zeros((8, 256 - span), F32)
        for j in range(PER_BATCH):
            k = b * PER_BATCH + j
            if k:
                ev_copy = copy(send_ev.at[b], ev.at[k], s_ev.at[k], r_ev.at[k], back(k))
                ev_copy.start()
                ev_sends.append(ev_copy)
            else:
                ev[0] = send_ev[0]
        for other in (1, 0):
            c = (core + other) % N_CORE
            r = resp[pl.ds(pl.multiple_of(c * h_rows, h_rows), h_rows), :]
            num = nn(r, batch)
            cnt = nt(r, chosen)
            if b:
                num += acc[c]
                cnt += racc[c]
            acc[c] = num
            racc[c] = cnt
            if b == batches - 1:
                own_lanes = iota((h_rows, 128), 1) // groups == (iota((h_rows, 128), 0) // (2 * per)) % N_YHI
                fold = jnp.where(own_lanes, cnt, 0.0).reshape(2, N_YHI, 2 * per, 128)
                fold = jnp.sum(fold, axis=1)
            if b == batches - 1 and other:
                rcore_out[...] = fold
                rc = copy(rcore_out, rcore_in, s_rcc, r_rcc, sibling)
                rc.start()
                core_sends.append(rc)
                x_rows = h_rows // 2
                for i, xp in enumerate((1 - pair, pair)):
                    at = pl.ds(pl.multiple_of(xp * x_rows, x_rows), x_rows)
                    cc = copy(acc.at[c, at], core_in.at[at], s_rsc.at[i], r_rsc.at[i], sibling)
                    cc.start()
                    core_sends.append(cc)

    core_sends[0].wait_recv()
    rx_out[...] = fold + rcore_in[...]
    x_sends = []
    for i, xp in enumerate((1 - pair, pair)):
        at = pl.ds(pl.multiple_of(xp * x_rows, x_rows), x_rows)
        core_sends[1 + i].wait_recv()
        both = acc[core, at] + core_in[at]
        if i:
            own_rows[...] = both
            continue
        x_out[...] = both.astype(BF16)
        xc = copy(x_out, x_in, s_rsx, r_rsx, x_peer)
        rc = copy(rx_out.at[xp], rx_in, s_rcx, r_rcx, x_peer)
        rc.start()
        xc.start()
        x_sends += [rc, xc]
    for c in x_sends:
        c.wait_recv()
    own_cnt = rx_out[pair] + rx_in[...]

    ry_out[...] = own_cnt
    y_sends = []
    for d in (2, 1, 3):
        at = pl.ds(pl.multiple_of(((y_hi + d) % N_YHI) * 2 * per, 2 * per), 2 * per)
        y_out[d - 1] = (own_rows[at] + x_in[at].astype(F32)).astype(BF16)
        yc = copy(y_out.at[d - 1], y_in.at[d - 1], s_rsy.at[d - 1], r_rsy.at[d - 1], y_peer(d))
        rc = copy(ry_out, ry_in.at[d - 1], s_rcy.at[d - 1], r_rcy.at[d - 1], y_peer(d))
        rc.start()
        yc.start()
        y_sends += [rc, yc]

    for c in ev_sends:
        c.wait_recv()
    at_lane = line_k - PER_BATCH * jnp.floor(line_k * (1.0 / PER_BATCH))
    lane_hot = (iota((256, rows), 0) == (at_lane * cap + rank).astype(jnp.int32)).astype(F32).astype(BF16)
    e_hi, e_mid, e_lo = three(ev[:, 0, :])
    by_target = nn(e_hi, lane_hot) + nn(e_mid, lane_hot) + nn(e_lo, lane_hot)
    line_ev[...] = jnp.sum(hot * by_target, axis=0, keepdims=True)

    at = pl.ds(pl.multiple_of(y_hi * 2 * per, 2 * per), 2 * per)
    part = own_rows[at] + x_in[at].astype(F32)
    for c in y_sends:
        c.wait_recv()
    for d in range(1, N_YHI):
        part += y_in[d - 1].astype(F32)
        own_cnt += ry_in[d - 1]
    fin_out[:, :, :width] = part.reshape(2, per, width)
    fin_out[:, :, width:] = own_cnt.reshape(2, per, 128)
    fin = copy(fin_out.at[1 - odd], fin_in.at[odd], s_fin.at[0], r_fin.at[odd], choose(near, across))
    fin.start()
    fin_2 = copy(fin_out.at[1], fin_in.at[1], s_fin.at[1], r_fin.at[1], beyond)

    @pl.when(odd == 1)
    def _():
        fin_2.start()
        copy(fin_out.at[0], fin_in.at[0], s_fin.at[0], r_fin.at[0], near).wait_recv()

    @pl.when(odd == 0)
    def _():
        fin_in[0] = fin_out[0]

    copy(fin_out.at[0], fin_in.at[1], s_fin.at[0], r_fin.at[1], near).wait_recv()
    final = fin_in[0] + fin_in[1]
    cnt = final[:, width:]
    cnt = jnp.where(iota(cnt.shape, 1) // groups == y_hi, cnt, 0.0)
    c_hi, c_mid, c_lo = three(cnt)
    den = nn(c_hi, ctf_sq4) + nn(c_mid, ctf_sq4) + nn(c_lo, ctf_sq4) + 1.0
    out[:, :half] = final[:, :half] / den
    out[:, half:] = final[:, half:width] / den

    @pl.when(odd == 1)
    def _():
        fin_2.wait_send()

    for c in sends + ev_sends + core_sends + x_sends + y_sends + [fin]:
        c.wait_send()


def on_device(images, references, ctf_table, ctf_ids, owners):
    rows, width = images.shape
    per = references.shape[0]
    n = len(OFFSETS)
    cap = 3 * rows // n
    h_rows = N_X * N_YHI * per
    x_rows = h_rows // 2
    dma = pltpu.SemaphoreType.DMA
    vm = pltpu.VMEM
    scratch = [
        vm((rows, width), BF16), vm((n, cap, width), BF16), vm((n, cap, width), BF16),
        vm((n, 8, 128), F32), vm((n, 8, 128), F32), vm((n // PER_BATCH, 8, 256), F32), vm((n, 8, 256), F32),
        vm((N_CORE, 2, N_YHI, 2, per, width), BF16), vm((N_CORE * h_rows, PER_BATCH * cap), BF16),
        vm((N_CORE * h_rows, 128), BF16), vm((N_CORE, h_rows, width), F32), vm((N_CORE, h_rows, 128), F32),
        vm((h_rows, width), F32), vm((2, 2 * per, 128), F32), vm((2, 2 * per, 128), F32),
        vm((x_rows, width), BF16), vm((x_rows, width), BF16), vm((2, 2 * per, 128), F32), vm((2 * per, 128), F32),
        vm((x_rows, width), F32),
        vm((N_YHI - 1, 2 * per, width), BF16), vm((N_YHI - 1, 2 * per, width), BF16),
        vm((2 * per, 128), F32), vm((N_YHI - 1, 2 * per, 128), F32),
        vm((2, per, width + 128), F32), vm((2, per, width + 128), F32),
        *[dma((n,))] * 6,
        *[dma((2,))] * 2, *[dma((N_YHI - 1,))] * 2, *[dma] * 2, *[dma((2,))] * 2,
        *[dma((2,))] * 2, *[dma] * 6, *[dma((N_YHI - 1,))] * 4,
        *[dma((2,))] * 2,
    ]
    new, ev = pl.pallas_call(
        kernel,
        out_shape=(jax.ShapeDtypeStruct((per, width), F32), jax.ShapeDtypeStruct((1, rows), F32)),
        in_specs=[pl.BlockSpec(memory_space=pltpu.VMEM)] * 5,
        out_specs=[pl.BlockSpec(memory_space=pltpu.VMEM)] * 2,
        scratch_shapes=scratch,
        compiler_params=pltpu.CompilerParams(
            collective_id=0, has_side_effects=True, vmem_limit_bytes=48 * 2**20
        ),
    )(images, references, ctf_table, ctf_ids.reshape(1, rows), owners.reshape(1, rows))
    return new, ev.reshape(rows)


def solution(mesh):
    both = P(("slab", "group"))
    rows = P(("slab", "group"), None)
    return jax.shard_map(
        on_device, mesh=mesh, in_specs=(rows, rows, P(), both, both), out_specs=(rows, both), check_vma=False
    )
```

```python
import functools

import jax
import jax.numpy as jnp
from jax import lax
from jax.experimental import pallas as pl
from jax.experimental.pallas import tpu as pltpu
from jax.sharding import PartitionSpec as P

F32, BF16 = jnp.float32, jnp.bfloat16
MESH = pl.DeviceIdType.MESH
N_X, N_Y, N_Z = 4, 8, 8
N_YLO, N_YHI, N_CORE = 2, 4, 2
FAR = N_Z // 2
OFFSETS = tuple((dz, dx * (1 - 2 * dy), dy) for dz in (0, 1, -1, 2) for dy in (0, 1) for dx in (0, 1))
PER_BATCH = 8


def nt(a, b):
    return lax.dot_general(a, b, (((1,), (1,)), ((), ())), preferred_element_type=F32)


def tn(a, b):
    return lax.dot_general(a, b, (((0,), (0,)), ((), ())), preferred_element_type=F32)


def nn(a, b):
    return jnp.dot(a, b, preferred_element_type=F32)


def three(v):
    hi = v.astype(BF16)
    rest = v - hi.astype(F32)
    mid = rest.astype(BF16)
    return hi, mid, (rest - mid.astype(F32)).astype(BF16)


def iota(shape, dim):
    return lax.broadcasted_iota(jnp.int32, shape, dim)


def kernel(
    img_hbm, refs_hbm, ctf_hbm, ids_hbm, own_hbm,
    out, line_ev,
    img, refs, ctf, ids, own,
    weighted, send_lines, lines, send_tags, tags, send_ev, ev,
    ref_all, resp, chosen, quad, acc, racc,
    core_in, rcore_out, rcore_in, x_out, x_in, rx_out, rx_in, own_rows, y_out, y_in, ry_out, ry_in,
    fin_out, fin_in, rfin_out, rfin_in,
    s_in,
    s_line, r_line, s_tag, r_tag, s_ev, r_ev,
    s_ag, r_ag, s_agy, r_agy, s_agx, r_agx, s_agc, r_agc,
    s_rsc, r_rsc, s_rcc, r_rcc, s_rsx, r_rsx, s_rcx, r_rcx, s_rsy, r_rsy, s_rcy, r_rcy,
    s_fin, r_fin, s_rfin, r_rfin,
):
    rows, width = img.shape
    per = refs.shape[0]
    half = width // 2
    groups = ctf.shape[0]
    n = len(OFFSETS)
    cap = 3 * rows // n
    batches = n // PER_BATCH
    span = PER_BATCH * cap
    slab, group = lax.axis_index("slab"), lax.axis_index("group")
    y_lo, z = slab // N_Z, slab % N_Z
    x, y_hi, core = group // (N_YHI * N_CORE), (group // N_CORE) % N_YHI, group % N_CORE
    y = N_YLO * y_hi + y_lo
    way = 1 - 2 * core
    odd, pair = x % 2, x // 2

    def device(dz, dx, dy):
        x_to, y_to, z_to = (x + dx + N_X) % N_X, (y + dy + N_Y) % N_Y, (z + dz + N_Z) % N_Z
        return (y_to % N_YLO) * N_Z + z_to, (x_to * N_YHI + y_to // N_YLO) * N_CORE + core

    def to(k):
        return device(*(way * d for d in OFFSETS[k]))

    def back(k):
        return device(*(-way * d for d in OFFSETS[k]))

    def slab_of(k):
        dz, dx, dy = (way * d for d in OFFSETS[k])
        return ((y + dy + N_Y) % N_YLO) * N_Z + (z + dz + N_Z + FAR * ((x + dx + N_X) % 2)) % N_Z

    def y_peer(d):
        return device(0, 0, N_YLO * d)

    x_peer = device(0, 2, 0)
    sibling = (slab, group + way)
    near, across, beyond = device(0, 1 - 2 * odd, 0), device(FAR, 1 - 2 * odd, 0), device(FAR, 0, 0)

    def choose(a, b):
        return tuple(odd * v + (1 - odd) * u for u, v in zip(a, b))

    def copy(src, dst, send, recv, device):
        return pltpu.make_async_remote_copy(
            src_ref=src, dst_ref=dst, send_sem=send, recv_sem=recv, device_id=device, device_id_type=MESH
        )

    loads = [
        pltpu.make_async_copy(a, b, s_in.at[i])
        for i, (a, b) in enumerate(((own_hbm, own), (ids_hbm, ids), (ctf_hbm, ctf), (refs_hbm, refs), (img_hbm, img)))
    ]
    for c in loads:
        c.start()

    barrier = pltpu.get_barrier_semaphore()
    partners = [back(k) for k in range(1, n)]
    partners += [y_peer(d) for d in range(1, N_YHI)] + [x_peer, sibling, near, across]
    for p in partners:
        pl.semaphore_signal(barrier, inc=1, device_id=p, device_id_type=MESH)

    @pl.when(odd == 1)
    def _():
        pl.semaphore_signal(barrier, inc=1, device_id=beyond, device_id_type=MESH)

    for c in loads[:3]:
        c.wait()

    target = iota((n, rows), 0)
    wanted = jnp.zeros((n, rows), jnp.int32)
    for k in range(n):
        wanted = jnp.where(target == k, slab_of(k), wanted)
    hot = (wanted == own[...]).astype(F32)
    hot_b = hot.astype(BF16)
    before = (iota((rows, rows), 0) < iota((rows, rows), 1)).astype(F32).astype(BF16)
    rank = jnp.sum(hot * nn(hot_b, before), axis=0, keepdims=True)
    line_k = jnp.sum(hot * target.astype(F32), axis=0, keepdims=True)
    slot = (line_k * cap + rank).astype(jnp.int32)
    tag_row = (ids[...] + 1).astype(F32)
    rank_hot = (iota((128, rows), 0) == rank.astype(jnp.int32)).astype(F32).astype(BF16)
    tag_slots = nt((hot * tag_row).astype(BF16), rank_hot)
    for k in range(n):
        send_tags[k] = jnp.broadcast_to(tag_slots[k : k + 1, :], (8, 128))

    pl.semaphore_wait(barrier, len(partners) + odd)
    loads[3].wait()

    slot_ref = ref_all.at[core, pair, y_hi, odd]
    ag = copy(refs, slot_ref, s_ag.at[0], r_ag.at[odd], choose(across, near))
    ag.start()
    ag_2 = copy(refs, slot_ref, s_ag.at[1], r_ag.at[1], beyond)

    @pl.when(odd == 1)
    def _():
        ag_2.start()

    @pl.when(odd == 0)
    def _():
        ref_all[core, pair, y_hi, 0] = refs[...]

    pick = (iota((groups, rows), 0) == ids[...]).astype(F32).astype(BF16)
    ctf_hi, ctf_mid, ctf_lo = three(ctf[...])
    ctf_rows = tn(pick, ctf_hi) + tn(pick, ctf_mid) + tn(pick, ctf_lo)
    loads[4].wait()
    weighted[:, :half] = (img[:, :half].astype(F32) * ctf_rows).astype(BF16)
    weighted[:, half:] = (img[:, half:].astype(F32) * ctf_rows).astype(BF16)

    @pl.when(odd == 1)
    def _():
        copy(refs, ref_all.at[core, pair, y_hi, 0], s_ag.at[0], r_ag.at[0], across).wait_recv()
        ag_2.wait_send()

    copy(refs, ref_all.at[core, pair, y_hi, 1], s_ag.at[0], r_ag.at[1], across).wait_recv()
    mine = ref_all.at[core, pair, y_hi]
    ag_y = [copy(mine, mine, s_agy.at[d - 1], r_agy.at[d - 1], y_peer(d)) for d in range(1, N_YHI)]
    for c in ag_y:
        c.start()
    sends = []
    for b in reversed(range(batches)):
        place = (iota((span, rows), 0) + b * span == slot).astype(F32).astype(BF16)
        packed = nn(place, weighted[...]).astype(BF16)
        for j in reversed(range(PER_BATCH)):
            k = b * PER_BATCH + j
            part = packed[j * cap : (j + 1) * cap]
            if k == 0:
                lines[0] = part
                tags[0] = send_tags[0]
                continue
            send_lines[k] = part
            line_copy = copy(send_lines.at[k], lines.at[k], s_line.at[k], r_line.at[k], to(k))
            tag_copy = copy(send_tags.at[k], tags.at[k], s_tag.at[k], r_tag.at[k], to(k))
            tag_copy.start()
            line_copy.start()
            sends += [tag_copy, line_copy]

    k_loc = N_CORE * N_X * N_YHI * per
    ctf_sq = ctf[...] * ctf[...]
    ctf_sq4 = jnp.concatenate([ctf_sq] * (128 // groups), axis=0).astype(BF16)
    p_rows = k_loc // 4

    def set_quad(c, p):
        reference = ref_all[c, p].reshape(p_rows, width)
        re, im = reference[:, :half].astype(F32), reference[:, half:].astype(F32)
        power = (re * re + im * im).astype(BF16)
        hi, mid, lo = three(-0.5 * nt(power, ctf_sq4))
        lane = iota((p_rows, 128), 1)
        parts = jnp.where(lane < 2 * groups, mid.astype(F32), jnp.where(lane < 3 * groups, lo.astype(F32), 0.0))
        quad[c, p] = jnp.where(lane < groups, hi.astype(F32), parts).astype(BF16)

    for c in ag_y:
        c.wait_recv()
    mine, theirs = ref_all.at[core, pair], ref_all.at[core, 1 - pair]
    ag_x = [copy(mine, mine, s_agx, r_agx, x_peer)]
    ag_x[0].start()
    ag_c = [copy(p, p, s_agc.at[i], r_agc.at[i], sibling) for i, p in enumerate((mine, theirs))]
    ag_c[0].start()
    set_quad(core, pair)
    ag_c[0].wait_recv()
    set_quad(1 - core, pair)
    ag_x[0].wait_recv()
    ag_c[1].start()
    set_quad(core, 1 - pair)
    ag_c[1].wait_recv()
    set_quad(1 - core, 1 - pair)
    sends += [ag] + ag_y + ag_x + ag_c

    scale = width**-0.5
    spread = (iota((128, span), 0) == iota((128, span), 1) % cap).astype(F32).astype(BF16)
    mine_8 = (iota((PER_BATCH * 8, span), 0) == 8 * (iota((PER_BATCH * 8, span), 1) // cap)).astype(F32)
    tag_of = (iota((128, span), 0) % groups + 1).astype(F32)
    ev_sends = []
    for b in range(batches):
        for j in range(PER_BATCH):
            k = b * PER_BATCH + j
            if k:
                copy(send_tags.at[k], tags.at[k], s_tag.at[k], r_tag.at[k], to(k)).wait_recv()
                copy(send_lines.at[k], lines.at[k], s_line.at[k], r_line.at[k], to(k)).wait_recv()
        here = slice(b * span, (b + 1) * span)
        batch = lines[b * PER_BATCH : (b + 1) * PER_BATCH].reshape(span, width)
        tag8 = tags[b * PER_BATCH : (b + 1) * PER_BATCH].reshape(PER_BATCH * 8, 128).astype(BF16)
        tag = jnp.sum(nn(tag8, spread) * mine_8, axis=0, keepdims=True)
        pick = (tag_of == tag).astype(F32).astype(BF16)
        chosen[:, here] = pick
        score = nt(ref_all[...].reshape(k_loc, width), batch) + nn(quad[...].reshape(k_loc, 128), pick)
        score *= scale
        top = jnp.max(score, axis=0, keepdims=True)
        e = jnp.exp(score - top)
        total = jnp.sum(e, axis=0, keepdims=True)
        resp[:, here] = (e * (1.0 / total)).astype(BF16)
        send_ev[b] = jnp.broadcast_to(top + jnp.log(total), (8, span))
        for j in range(PER_BATCH):
            k = b * PER_BATCH + j
            if k:
                ev_copy = copy(send_ev.at[b], ev.at[k], s_ev.at[k], r_ev.at[k], back(k))
                ev_copy.start()
                ev_sends.append(ev_copy)
            else:
                ev[0] = send_ev[0]

    h_rows = k_loc // N_CORE
    x_rows = h_rows // 2
    own_lanes = iota((h_rows, 128), 1) // groups == (iota((h_rows, 128), 0) // 8) % (2 * per // 8)

    def sum_half(c):
        r = resp[pl.ds(pl.multiple_of(c * h_rows, h_rows), h_rows), :]
        acc[c] = nn(r, lines[...].reshape(n * cap, width))
        count = jnp.where(own_lanes, nt(r, chosen[...]), 0.0)
        return jnp.sum(count.reshape(2, N_YHI, 2 * per // 8, 8, 128), axis=2)

    rcore_out[...] = sum_half(1 - core)
    core_sends = [copy(rcore_out, rcore_in, s_rcc, r_rcc, sibling)]
    for i, xp in enumerate((1 - pair, pair)):
        at = pl.ds(pl.multiple_of(xp * x_rows, x_rows), x_rows)
        core_sends.append(copy(acc.at[1 - core, at], core_in.at[at], s_rsc.at[i], r_rsc.at[i], sibling))
    for c in core_sends:
        c.start()
    racc[...] = sum_half(core)

    core_sends[0].wait_recv()
    rx_out[...] = racc[...] + rcore_in[...]
    x_sends = []
    for i, xp in enumerate((1 - pair, pair)):
        at = pl.ds(pl.multiple_of(xp * x_rows, x_rows), x_rows)
        core_sends[1 + i].wait_recv()
        both = acc[core, at] + core_in[at]
        if i:
            own_rows[...] = both
            continue
        x_out[...] = both.astype(BF16)
        xc = copy(x_out, x_in, s_rsx, r_rsx, x_peer)
        rc = copy(rx_out.at[xp], rx_in, s_rcx, r_rcx, x_peer)
        rc.start()
        xc.start()
        x_sends += [rc, xc]
    for c in x_sends:
        c.wait_recv()
    own_cnt = rx_out[pair] + rx_in[...]

    ry_out[...] = own_cnt
    y_sends = []
    for d in (2, 1, 3):
        at = pl.ds(pl.multiple_of(((y_hi + d) % N_YHI) * 2 * per, 2 * per), 2 * per)
        y_out[d - 1] = (own_rows[at] + x_in[at].astype(F32)).astype(BF16)
        yc = copy(y_out.at[d - 1], y_in.at[d - 1], s_rsy.at[d - 1], r_rsy.at[d - 1], y_peer(d))
        rc = copy(ry_out.at[(y_hi + d) % N_YHI], ry_in.at[d - 1], s_rcy.at[d - 1], r_rcy.at[d - 1], y_peer(d))
        rc.start()
        yc.start()
        y_sends += [rc, yc]

    for c in ev_sends:
        c.wait_recv()
    at_lane = line_k - PER_BATCH * jnp.floor(line_k * (1.0 / PER_BATCH))
    lane_hot = (iota((span, rows), 0) == (at_lane * cap + rank).astype(jnp.int32)).astype(F32).astype(BF16)
    e_hi, e_mid, e_lo = three(ev[:, 0, :])
    by_target = nn(e_hi, lane_hot) + nn(e_mid, lane_hot) + nn(e_lo, lane_hot)
    line_ev[...] = jnp.sum(hot * by_target, axis=0, keepdims=True)

    at = pl.ds(pl.multiple_of(y_hi * 2 * per, 2 * per), 2 * per)
    part = own_rows[at] + x_in[at].astype(F32)
    for c in y_sends:
        c.wait_recv()
    count = ry_out[y_hi]
    for d in range(1, N_YHI):
        part += y_in[d - 1].astype(F32)
        count += ry_in[d - 1]
    fin_out[...] = part.reshape(2, per, width).astype(BF16)
    rfin_out[...] = count

    def fins(src, dst, i, dev):
        return (
            copy(rfin_out, rfin_in.at[dst], s_rfin.at[i], r_rfin.at[dst], dev),
            copy(fin_out.at[src], fin_in.at[dst], s_fin.at[i], r_fin.at[dst], dev),
        )

    fin = fins(1 - odd, odd, 0, choose(near, across))
    fin_2 = fins(1, 1, 1, beyond)
    for c in fin:
        c.start()

    @pl.when(odd == 1)
    def _():
        for c in fin_2:
            c.start()
        for c in fins(0, 0, 0, near):
            c.wait_recv()

    @pl.when(odd == 0)
    def _():
        fin_in[0] = fin_out[0]
        rfin_in[0] = rfin_out[...]

    for c in fins(0, 1, 0, near):
        c.wait_recv()
    final = fin_in[0].astype(F32) + fin_in[1].astype(F32)
    tile = rfin_in[0] + rfin_in[1]
    cnt = jnp.concatenate([tile] * (per // 8), axis=0)
    cnt = jnp.where(iota((per, 128), 1) // groups == iota((per, 128), 0) // 8 + odd * (per // 8), cnt, 0.0)
    c_hi, c_mid, c_lo = three(cnt)
    den = nn(c_hi, ctf_sq4) + nn(c_mid, ctf_sq4) + nn(c_lo, ctf_sq4) + 1.0
    out[:, :half] = final[:, :half] / den
    out[:, half:] = final[:, half:] / den

    @pl.when(odd == 1)
    def _():
        for c in fin_2:
            c.wait_send()

    for c in sends + ev_sends + core_sends + x_sends + y_sends + list(fin):
        c.wait_send()


def on_device(images, references, ctf_table, ctf_ids, owners):
    rows, width = images.shape
    per = references.shape[0]
    n = len(OFFSETS)
    cap = 3 * rows // n
    h_rows = N_X * N_YHI * per
    x_rows = h_rows // 2
    dma = pltpu.SemaphoreType.DMA
    vm = pltpu.VMEM
    scratch = [
        vm((rows, width), BF16), vm((per, width), BF16), vm(ctf_table.shape, F32),
        vm((1, rows), jnp.int32), vm((1, rows), jnp.int32),
        vm((rows, width), BF16), vm((n, cap, width), BF16), vm((n, cap, width), BF16),
        vm((n, 8, 128), F32), vm((n, 8, 128), F32),
        vm((n // PER_BATCH, 8, PER_BATCH * cap), F32), vm((n, 8, PER_BATCH * cap), F32),
        vm((N_CORE, 2, N_YHI, 2, per, width), BF16), vm((N_CORE * h_rows, n * cap), BF16), vm((128, n * cap), BF16),
        vm((N_CORE, 2, x_rows, 128), BF16), vm((N_CORE, h_rows, width), F32), vm((2, N_YHI, 8, 128), F32),
        vm((h_rows, width), F32), vm((2, N_YHI, 8, 128), F32), vm((2, N_YHI, 8, 128), F32),
        vm((x_rows, width), BF16), vm((x_rows, width), BF16), vm((2, N_YHI, 8, 128), F32), vm((N_YHI, 8, 128), F32),
        vm((x_rows, width), F32),
        vm((N_YHI - 1, 2 * per, width), BF16), vm((N_YHI - 1, 2 * per, width), BF16),
        vm((N_YHI, 8, 128), F32), vm((N_YHI - 1, 8, 128), F32),
        vm((2, per, width), BF16), vm((2, per, width), BF16), vm((8, 128), F32), vm((2, 8, 128), F32),
        dma((5,)),
        *[dma((n,))] * 6,
        *[dma((2,))] * 2, *[dma((N_YHI - 1,))] * 2, *[dma] * 2, *[dma((2,))] * 2,
        *[dma((2,))] * 2, *[dma] * 6, *[dma((N_YHI - 1,))] * 4,
        *[dma((2,))] * 4,
    ]
    new, ev = pl.pallas_call(
        kernel,
        out_shape=(jax.ShapeDtypeStruct((per, width), F32), jax.ShapeDtypeStruct((1, rows), F32)),
        in_specs=[pl.BlockSpec(memory_space=pltpu.HBM)] * 5,
        out_specs=[pl.BlockSpec(memory_space=pltpu.VMEM)] * 2,
        scratch_shapes=scratch,
        compiler_params=pltpu.CompilerParams(
            collective_id=0, has_side_effects=True, vmem_limit_bytes=48 * 2**20
        ),
    )(images, references, ctf_table, ctf_ids.reshape(1, rows), owners.reshape(1, rows))
    return new, ev.reshape(rows)


def solution(mesh):
    both = P(("slab", "group"))
    rows = P(("slab", "group"), None)
    return jax.shard_map(
        on_device, mesh=mesh, in_specs=(rows, rows, P(), both, both), out_specs=(rows, both), check_vma=False
    )
```

```python
import functools

import jax
import jax.numpy as jnp
from jax import lax
from jax.experimental import pallas as pl
from jax.experimental.pallas import tpu as pltpu
from jax.sharding import PartitionSpec as P

F32, BF16 = jnp.float32, jnp.bfloat16
MESH = pl.DeviceIdType.MESH
N_X, N_Y, N_Z = 4, 8, 8
N_YLO, N_YHI, N_CORE = 2, 4, 2
FAR = N_Z // 2
OFFSETS = tuple((dz, dx * (1 - 2 * dy), dy) for dz in (0, 1, -1, 2) for dy in (0, 1) for dx in (0, 1))
PER_BATCH = 8


def nt(a, b):
    return lax.dot_general(a, b, (((1,), (1,)), ((), ())), preferred_element_type=F32)


def tn(a, b):
    return lax.dot_general(a, b, (((0,), (0,)), ((), ())), preferred_element_type=F32)


def nn(a, b):
    return jnp.dot(a, b, preferred_element_type=F32)


def three(v):
    hi = v.astype(BF16)
    rest = v - hi.astype(F32)
    mid = rest.astype(BF16)
    return hi, mid, (rest - mid.astype(F32)).astype(BF16)


def iota(shape, dim):
    return lax.broadcasted_iota(jnp.int32, shape, dim)


def kernel(
    img_hbm, refs_hbm, ctf_hbm, ids_hbm, own_hbm,
    out, line_ev,
    img, refs, ctf, ids, own,
    weighted, send_lines, lines, send_tags, tags, send_ev, ev,
    ref_all, resp, chosen, quad, acc, racc,
    core_in, rcore_out, rcore_in, x_out, x_in, rx_out, rx_in, own_rows, y_out, y_in, ry_out, ry_in,
    fin_out, fin_in, rfin_out, rfin_in,
    s_in,
    s_line, r_line, s_tag, r_tag, s_ev, r_ev,
    s_ag, r_ag, s_agy, r_agy, s_agx, r_agx, s_agc, r_agc,
    s_rsc, r_rsc, s_rcc, r_rcc, s_rsx, r_rsx, s_rcx, r_rcx, s_rsy, r_rsy, s_rcy, r_rcy,
    s_fin, r_fin, s_rfin, r_rfin,
):
    rows, width = img.shape
    per = refs.shape[0]
    half = width // 2
    groups = ctf.shape[0]
    n = len(OFFSETS)
    cap = 3 * rows // n
    batches = n // PER_BATCH
    span = PER_BATCH * cap
    slab, group = lax.axis_index("slab"), lax.axis_index("group")
    y_lo, z = slab // N_Z, slab % N_Z
    x, y_hi, core = group // (N_YHI * N_CORE), (group // N_CORE) % N_YHI, group % N_CORE
    y = N_YLO * y_hi + y_lo
    way = 1 - 2 * core
    odd, pair = x % 2, x // 2

    def device(dz, dx, dy):
        x_to, y_to, z_to = (x + dx + N_X) % N_X, (y + dy + N_Y) % N_Y, (z + dz + N_Z) % N_Z
        return (y_to % N_YLO) * N_Z + z_to, (x_to * N_YHI + y_to // N_YLO) * N_CORE + core

    def to(k):
        return device(*(way * d for d in OFFSETS[k]))

    def back(k):
        return device(*(-way * d for d in OFFSETS[k]))

    def slab_of(k):
        dz, dx, dy = (way * d for d in OFFSETS[k])
        return ((y + dy + N_Y) % N_YLO) * N_Z + (z + dz + N_Z + FAR * ((x + dx + N_X) % 2)) % N_Z

    def y_peer(d):
        return device(0, 0, N_YLO * d)

    x_peer = device(0, 2, 0)
    sibling = (slab, group + way)
    near, across, beyond = device(0, 1 - 2 * odd, 0), device(FAR, 1 - 2 * odd, 0), device(FAR, 0, 0)

    def choose(a, b):
        return tuple(odd * v + (1 - odd) * u for u, v in zip(a, b))

    def copy(src, dst, send, recv, device):
        return pltpu.make_async_remote_copy(
            src_ref=src, dst_ref=dst, send_sem=send, recv_sem=recv, device_id=device, device_id_type=MESH
        )

    loads = [
        pltpu.make_async_copy(a, b, s_in.at[i])
        for i, (a, b) in enumerate(((own_hbm, own), (ids_hbm, ids), (ctf_hbm, ctf), (refs_hbm, refs), (img_hbm, img)))
    ]
    for c in loads:
        c.start()

    barrier = pltpu.get_barrier_semaphore()
    partners = [back(k) for k in range(1, n)]
    partners += [y_peer(d) for d in range(1, N_YHI)] + [x_peer, sibling, near, across]
    for p in partners:
        pl.semaphore_signal(barrier, inc=1, device_id=p, device_id_type=MESH)

    @pl.when(odd == 1)
    def _():
        pl.semaphore_signal(barrier, inc=1, device_id=beyond, device_id_type=MESH)

    for c in loads[:3]:
        c.wait()

    target = iota((n, rows), 0)
    wanted = jnp.zeros((n, rows), jnp.int32)
    for k in range(n):
        wanted = jnp.where(target == k, slab_of(k), wanted)
    hot = (wanted == own[...]).astype(F32)
    hot_b = hot.astype(BF16)
    before = (iota((rows, rows), 0) < iota((rows, rows), 1)).astype(F32).astype(BF16)
    rank = jnp.sum(hot * nn(hot_b, before), axis=0, keepdims=True)
    line_k = jnp.sum(hot * target.astype(F32), axis=0, keepdims=True)
    slot = (line_k * cap + rank).astype(jnp.int32)
    tag_row = (ids[...] + 1).astype(F32)
    rank_hot = (iota((128, rows), 0) == rank.astype(jnp.int32)).astype(F32).astype(BF16)
    tag_slots = nt((hot * tag_row).astype(BF16), rank_hot)
    for k in range(n):
        send_tags[k] = jnp.broadcast_to(tag_slots[k : k + 1, :], (8, 128))

    pl.semaphore_wait(barrier, len(partners) + odd)
    loads[3].wait()

    slot_ref = ref_all.at[core, pair, y_hi, odd]
    ag = copy(refs, slot_ref, s_ag.at[0], r_ag.at[odd], choose(across, near))
    ag.start()
    ag_2 = copy(refs, slot_ref, s_ag.at[1], r_ag.at[1], beyond)

    @pl.when(odd == 1)
    def _():
        ag_2.start()

    @pl.when(odd == 0)
    def _():
        ref_all[core, pair, y_hi, 0] = refs[...]

    pick = (iota((groups, rows), 0) == ids[...]).astype(F32).astype(BF16)
    ctf_hi, ctf_mid, ctf_lo = three(ctf[...])
    ctf_rows = tn(pick, ctf_hi) + tn(pick, ctf_mid) + tn(pick, ctf_lo)
    loads[4].wait()
    weighted[:, :half] = (img[:, :half].astype(F32) * ctf_rows).astype(BF16)
    weighted[:, half:] = (img[:, half:].astype(F32) * ctf_rows).astype(BF16)

    @pl.when(odd == 1)
    def _():
        copy(refs, ref_all.at[core, pair, y_hi, 0], s_ag.at[0], r_ag.at[0], across).wait_recv()
        ag_2.wait_send()

    copy(refs, ref_all.at[core, pair, y_hi, 1], s_ag.at[0], r_ag.at[1], across).wait_recv()
    mine = ref_all.at[core, pair, y_hi]
    ag_y = [copy(mine, mine, s_agy.at[d - 1], r_agy.at[d - 1], y_peer(d)) for d in range(1, N_YHI)]
    for c in ag_y:
        c.start()
    blocks = [ref_all.at[core, pair, (y_hi + N_YHI - d) % N_YHI] for d in range(N_YHI)]
    ag_x = [copy(p, p, s_agx.at[d], r_agx.at[d], x_peer) for d, p in enumerate(blocks)]
    ag_x[0].start()

    sends = []
    for b in reversed(range(batches)):
        place = (iota((span, rows), 0) + b * span == slot).astype(F32).astype(BF16)
        packed = nn(place, weighted[...]).astype(BF16)
        for j in reversed(range(PER_BATCH)):
            k = b * PER_BATCH + j
            part = packed[j * cap : (j + 1) * cap]
            if k == 0:
                lines[0] = part
                tags[0] = send_tags[0]
                continue
            send_lines[k] = part
            line_copy = copy(send_lines.at[k], lines.at[k], s_line.at[k], r_line.at[k], to(k))
            tag_copy = copy(send_tags.at[k], tags.at[k], s_tag.at[k], r_tag.at[k], to(k))
            tag_copy.start()
            line_copy.start()
            sends += [tag_copy, line_copy]

    k_loc = N_CORE * N_X * N_YHI * per
    ctf_sq = ctf[...] * ctf[...]
    ctf_sq4 = jnp.concatenate([ctf_sq] * (128 // groups), axis=0).astype(BF16)
    p_rows = k_loc // 4

    def set_quad(c, p):
        reference = ref_all[c, p].reshape(p_rows, width)
        re, im = reference[:, :half].astype(F32), reference[:, half:].astype(F32)
        power = (re * re + im * im).astype(BF16)
        hi, mid, lo = three(-0.5 * nt(power, ctf_sq4))
        lane = iota((p_rows, 128), 1)
        parts = jnp.where(lane < 2 * groups, mid.astype(F32), jnp.where(lane < 3 * groups, lo.astype(F32), 0.0))
        quad[c, p] = jnp.where(lane < groups, hi.astype(F32), parts).astype(BF16)

    for d in (1, 3, 2):
        ag_y[d - 1].wait_recv()
        ag_x[d].start()
    mine, theirs = ref_all.at[core, pair], ref_all.at[core, 1 - pair]
    ag_c = [copy(p, p, s_agc.at[i], r_agc.at[i], sibling) for i, p in enumerate((mine, theirs))]
    ag_c[0].start()
    set_quad(core, pair)
    ag_c[0].wait_recv()
    set_quad(1 - core, pair)
    for c in ag_x:
        c.wait_recv()
    ag_c[1].start()
    set_quad(core, 1 - pair)
    ag_c[1].wait_recv()
    set_quad(1 - core, 1 - pair)
    sends += [ag] + ag_y + ag_x + ag_c

    scale = width**-0.5
    spread = (iota((128, span), 0) == iota((128, span), 1) % cap).astype(F32).astype(BF16)
    mine_8 = (iota((PER_BATCH * 8, span), 0) == 8 * (iota((PER_BATCH * 8, span), 1) // cap)).astype(F32)
    tag_of = (iota((128, span), 0) % groups + 1).astype(F32)
    ev_sends = []
    for b in range(batches):
        for j in range(PER_BATCH):
            k = b * PER_BATCH + j
            if k:
                copy(send_tags.at[k], tags.at[k], s_tag.at[k], r_tag.at[k], to(k)).wait_recv()
                copy(send_lines.at[k], lines.at[k], s_line.at[k], r_line.at[k], to(k)).wait_recv()
        here = slice(b * span, (b + 1) * span)
        batch = lines[b * PER_BATCH : (b + 1) * PER_BATCH].reshape(span, width)
        tag8 = tags[b * PER_BATCH : (b + 1) * PER_BATCH].reshape(PER_BATCH * 8, 128).astype(BF16)
        tag = jnp.sum(nn(tag8, spread) * mine_8, axis=0, keepdims=True)
        pick = (tag_of == tag).astype(F32).astype(BF16)
        chosen[:, here] = pick
        score = nt(ref_all[...].reshape(k_loc, width), batch) + nn(quad[...].reshape(k_loc, 128), pick)
        score *= scale
        top = jnp.max(score, axis=0, keepdims=True)
        e = jnp.exp(score - top)
        total = jnp.sum(e, axis=0, keepdims=True)
        resp[:, here] = (e * (1.0 / total)).astype(BF16)
        send_ev[b] = top + jnp.log(total)
        for j in range(PER_BATCH):
            k = b * PER_BATCH + j
            if k:
                ev_copy = copy(send_ev.at[b], ev.at[k], s_ev.at[k], r_ev.at[k], back(k))
                ev_copy.start()
                ev_sends.append(ev_copy)
            else:
                ev[0] = send_ev[0]

    h_rows = k_loc // N_CORE
    x_rows = h_rows // 2
    own_lanes = iota((h_rows, 128), 1) // groups == (iota((h_rows, 128), 0) // 8) % (2 * per // 8)

    def sum_half(c):
        r = resp[pl.ds(pl.multiple_of(c * h_rows, h_rows), h_rows), :]
        acc[c] = nn(r, lines[...].reshape(n * cap, width))
        count = jnp.where(own_lanes, nt(r, chosen[...]), 0.0)
        return jnp.sum(count.reshape(2, N_YHI, 2 * per // 8, 8, 128), axis=2)

    rcore_out[...] = sum_half(1 - core)
    core_sends = [copy(rcore_out, rcore_in, s_rcc, r_rcc, sibling)]
    for i, xp in enumerate((1 - pair, pair)):
        at = pl.ds(pl.multiple_of(xp * x_rows, x_rows), x_rows)
        core_sends.append(copy(acc.at[1 - core, at], core_in.at[at], s_rsc.at[i], r_rsc.at[i], sibling))
    for c in core_sends:
        c.start()
    racc[...] = sum_half(core)

    core_sends[0].wait_recv()
    rx_out[...] = racc[...] + rcore_in[...]
    rc = copy(rx_out.at[1 - pair], rx_in, s_rcx, r_rcx, x_peer)
    rc.start()
    x_sends = []
    turns = (2, 1, 3, 0)
    core_sends[1].wait_recv()

    def rows_of(d, first=0):
        at = first + ((y_hi + d) % N_YHI) * 2 * per
        return pl.ds(pl.multiple_of(at, 2 * per), 2 * per)

    for i, d in enumerate(turns):
        at, far_at = rows_of(d), rows_of(d, (1 - pair) * x_rows)
        x_out[at] = (acc[core, far_at] + core_in[far_at]).astype(BF16)
        x_sends.append(copy(x_out.at[at], x_in.at[at], s_rsx.at[i], r_rsx.at[i], x_peer))
        x_sends[-1].start()
    core_sends[2].wait_recv()
    near_at = pl.ds(pl.multiple_of(pair * x_rows, x_rows), x_rows)
    own_rows[...] = acc[core, near_at] + core_in[near_at]

    rc.wait_recv()
    own_cnt = rx_out[pair] + rx_in[...]
    ry_out[...] = own_cnt
    y_sends = []
    for i, d in enumerate(turns[:-1]):
        x_sends[i].wait_recv()
        at = rows_of(d)
        y_out[d - 1] = (own_rows[at] + x_in[at].astype(F32)).astype(BF16)
        yc = copy(y_out.at[d - 1], y_in.at[d - 1], s_rsy.at[d - 1], r_rsy.at[d - 1], y_peer(d))
        rcy = copy(ry_out.at[(y_hi + d) % N_YHI], ry_in.at[d - 1], s_rcy.at[d - 1], r_rcy.at[d - 1], y_peer(d))
        rcy.start()
        yc.start()
        y_sends += [rcy, yc]
    x_sends[-1].wait_recv()
    x_sends.append(rc)

    for c in ev_sends:
        c.wait_recv()
    at_lane = line_k - PER_BATCH * jnp.floor(line_k * (1.0 / PER_BATCH))
    lane_hot = (iota((span, rows), 0) == (at_lane * cap + rank).astype(jnp.int32)).astype(F32).astype(BF16)
    e_hi, e_mid, e_lo = three(ev[:, 0, :])
    by_target = nn(e_hi, lane_hot) + nn(e_mid, lane_hot) + nn(e_lo, lane_hot)
    line_ev[...] = jnp.sum(hot * by_target, axis=0, keepdims=True)

    at = rows_of(0)
    part = own_rows[at] + x_in[at].astype(F32)
    for c in y_sends:
        c.wait_recv()
    count = ry_out[y_hi]
    for d in range(1, N_YHI):
        part += y_in[d - 1].astype(F32)
        count += ry_in[d - 1]
    fin_out[...] = part.reshape(2, per, width).astype(BF16)
    rfin_out[...] = count

    def fins(src, dst, i, dev):
        return (
            copy(rfin_out, rfin_in.at[dst], s_rfin.at[i], r_rfin.at[dst], dev),
            copy(fin_out.at[src], fin_in.at[dst], s_fin.at[i], r_fin.at[dst], dev),
        )

    fin = fins(1 - odd, odd, 0, choose(near, across))
    fin_2 = fins(1, 1, 1, beyond)
    for c in fin:
        c.start()

    @pl.when(odd == 1)
    def _():
        for c in fin_2:
            c.start()
        for c in fins(0, 0, 0, near):
            c.wait_recv()

    @pl.when(odd == 0)
    def _():
        fin_in[0] = fin_out[0]
        rfin_in[0] = rfin_out[...]

    for c in fins(0, 1, 0, near):
        c.wait_recv()
    final = fin_in[0].astype(F32) + fin_in[1].astype(F32)
    tile = rfin_in[0] + rfin_in[1]
    cnt = jnp.concatenate([tile] * (per // 8), axis=0)
    cnt = jnp.where(iota((per, 128), 1) // groups == iota((per, 128), 0) // 8 + odd * (per // 8), cnt, 0.0)
    c_hi, c_mid, c_lo = three(cnt)
    den = nn(c_hi, ctf_sq4) + nn(c_mid, ctf_sq4) + nn(c_lo, ctf_sq4) + 1.0
    out[:, :half] = final[:, :half] / den
    out[:, half:] = final[:, half:] / den

    @pl.when(odd == 1)
    def _():
        for c in fin_2:
            c.wait_send()

    for c in sends + ev_sends + core_sends + x_sends + y_sends + list(fin):
        c.wait_send()


def on_device(images, references, ctf_table, ctf_ids, owners):
    rows, width = images.shape
    per = references.shape[0]
    n = len(OFFSETS)
    cap = 3 * rows // n
    h_rows = N_X * N_YHI * per
    x_rows = h_rows // 2
    dma = pltpu.SemaphoreType.DMA
    vm = pltpu.VMEM
    scratch = [
        vm((rows, width), BF16), vm((per, width), BF16), vm(ctf_table.shape, F32),
        vm((1, rows), jnp.int32), vm((1, rows), jnp.int32),
        vm((rows, width), BF16), vm((n, cap, width), BF16), vm((n, cap, width), BF16),
        vm((n, 8, 128), F32), vm((n, 8, 128), F32),
        vm((n // PER_BATCH, 1, PER_BATCH * cap), F32), vm((n, 1, PER_BATCH * cap), F32),
        vm((N_CORE, 2, N_YHI, 2, per, width), BF16), vm((N_CORE * h_rows, n * cap), BF16), vm((128, n * cap), BF16),
        vm((N_CORE, 2, x_rows, 128), BF16), vm((N_CORE, h_rows, width), F32), vm((2, N_YHI, 8, 128), F32),
        vm((h_rows, width), F32), vm((2, N_YHI, 8, 128), F32), vm((2, N_YHI, 8, 128), F32),
        vm((x_rows, width), BF16), vm((x_rows, width), BF16), vm((2, N_YHI, 8, 128), F32), vm((N_YHI, 8, 128), F32),
        vm((x_rows, width), F32),
        vm((N_YHI - 1, 2 * per, width), BF16), vm((N_YHI - 1, 2 * per, width), BF16),
        vm((N_YHI, 8, 128), F32), vm((N_YHI - 1, 8, 128), F32),
        vm((2, per, width), BF16), vm((2, per, width), BF16), vm((8, 128), F32), vm((2, 8, 128), F32),
        dma((5,)),
        *[dma((n,))] * 6,
        *[dma((2,))] * 2, *[dma((N_YHI - 1,))] * 2, *[dma((N_YHI,))] * 2, *[dma((2,))] * 2,
        *[dma((2,))] * 2, *[dma] * 2, *[dma((N_YHI,))] * 2, *[dma] * 2, *[dma((N_YHI - 1,))] * 4,
        *[dma((2,))] * 4,
    ]
    new, ev = pl.pallas_call(
        kernel,
        out_shape=(jax.ShapeDtypeStruct((per, width), F32), jax.ShapeDtypeStruct((1, rows), F32)),
        in_specs=[pl.BlockSpec(memory_space=pltpu.HBM)] * 5,
        out_specs=[pl.BlockSpec(memory_space=pltpu.VMEM)] * 2,
        scratch_shapes=scratch,
        compiler_params=pltpu.CompilerParams(
            collective_id=0, has_side_effects=True, vmem_limit_bytes=62 * 2**20
        ),
    )(images, references, ctf_table, ctf_ids.reshape(1, rows), owners.reshape(1, rows))
    return new, ev.reshape(rows)


def solution(mesh):
    both = P(("slab", "group"))
    rows = P(("slab", "group"), None)
    return jax.shard_map(
        on_device, mesh=mesh, in_specs=(rows, rows, P(), both, both), out_specs=(rows, both), check_vma=False
    )
```

```python
import functools

import jax
import jax.numpy as jnp
from jax import lax
from jax.experimental import pallas as pl
from jax.experimental.pallas import tpu as pltpu
from jax.sharding import PartitionSpec as P

F32, BF16 = jnp.float32, jnp.bfloat16
MESH = pl.DeviceIdType.MESH
N_X, N_Y, N_Z = 4, 8, 8
N_YLO, N_YHI, N_CORE = 2, 4, 2
FAR = N_Z // 2
OFFSETS = tuple((dz, dx * (1 - 2 * dy), dy) for dz in (0, 1, -1, 2) for dy in (0, 1) for dx in (0, 1))
PER_BATCH = 8


def nt(a, b):
    return lax.dot_general(a, b, (((1,), (1,)), ((), ())), preferred_element_type=F32)


def tn(a, b):
    return lax.dot_general(a, b, (((0,), (0,)), ((), ())), preferred_element_type=F32)


def nn(a, b):
    return jnp.dot(a, b, preferred_element_type=F32)


def three(v):
    hi = v.astype(BF16)
    rest = v - hi.astype(F32)
    mid = rest.astype(BF16)
    return hi, mid, (rest - mid.astype(F32)).astype(BF16)


def iota(shape, dim):
    return lax.broadcasted_iota(jnp.int32, shape, dim)


def kernel(
    img_hbm, refs_hbm, ctf_hbm, ids_hbm, own_hbm,
    out, line_ev,
    img, refs, ctf, ids, own,
    weighted, send_lines, lines, send_tags, tags, send_ev, ev,
    ref_all, resp, chosen, quad, acc, racc,
    core_in, rcore_out, rcore_in, x_out, x_in, rx_out, rx_in, own_rows, y_out, y_in, ry_out, ry_in,
    fin_out, fin_in, rfin_out, rfin_in,
    s_in,
    s_line, r_line, s_tag, r_tag, s_ev, r_ev,
    s_ag, r_ag, s_agy, r_agy, s_agx, r_agx, s_agc, r_agc,
    s_rsc, r_rsc, s_rcc, r_rcc, s_rsx, r_rsx, s_rcx, r_rcx, s_rsy, r_rsy, s_rcy, r_rcy,
    s_fin, r_fin, s_rfin, r_rfin,
):
    rows, width = img.shape
    per = refs.shape[0]
    half = width // 2
    groups = ctf.shape[0]
    n = len(OFFSETS)
    cap = 3 * rows // n
    batches = n // PER_BATCH
    span = PER_BATCH * cap
    slab, group = lax.axis_index("slab"), lax.axis_index("group")
    y_lo, z = slab // N_Z, slab % N_Z
    x, y_hi, core = group // (N_YHI * N_CORE), (group // N_CORE) % N_YHI, group % N_CORE
    y = N_YLO * y_hi + y_lo
    way = 1 - 2 * core
    odd, pair = x % 2, x // 2

    def device(dz, dx, dy):
        x_to, y_to, z_to = (x + dx + N_X) % N_X, (y + dy + N_Y) % N_Y, (z + dz + N_Z) % N_Z
        return (y_to % N_YLO) * N_Z + z_to, (x_to * N_YHI + y_to // N_YLO) * N_CORE + core

    def to(k):
        return device(*(way * d for d in OFFSETS[k]))

    def back(k):
        return device(*(-way * d for d in OFFSETS[k]))

    def slab_of(k):
        dz, dx, dy = (way * d for d in OFFSETS[k])
        return ((y + dy + N_Y) % N_YLO) * N_Z + (z + dz + N_Z + FAR * ((x + dx + N_X) % 2)) % N_Z

    def y_peer(d):
        return device(0, 0, N_YLO * d)

    x_peer = device(0, 2, 0)
    sibling = (slab, group + way)
    near, across, beyond = device(0, 1 - 2 * odd, 0), device(FAR, 1 - 2 * odd, 0), device(FAR, 0, 0)

    def choose(a, b):
        return tuple(odd * v + (1 - odd) * u for u, v in zip(a, b))

    def copy(src, dst, send, recv, device):
        return pltpu.make_async_remote_copy(
            src_ref=src, dst_ref=dst, send_sem=send, recv_sem=recv, device_id=device, device_id_type=MESH
        )

    loads = [
        pltpu.make_async_copy(a, b, s_in.at[i])
        for i, (a, b) in enumerate(((own_hbm, own), (ids_hbm, ids), (ctf_hbm, ctf), (refs_hbm, refs), (img_hbm, img)))
    ]
    for c in loads:
        c.start()

    barrier = pltpu.get_barrier_semaphore()
    partners = [back(k) for k in range(1, n)]
    partners += [y_peer(d) for d in range(1, N_YHI)] + [x_peer, sibling, near, across]
    for p in partners:
        pl.semaphore_signal(barrier, inc=1, device_id=p, device_id_type=MESH)

    @pl.when(odd == 1)
    def _():
        pl.semaphore_signal(barrier, inc=1, device_id=beyond, device_id_type=MESH)

    for c in loads[:3]:
        c.wait()

    target = iota((n, rows), 0)
    wanted = jnp.zeros((n, rows), jnp.int32)
    for k in range(n):
        wanted = jnp.where(target == k, slab_of(k), wanted)
    hot = (wanted == own[...]).astype(F32)
    hot_b = hot.astype(BF16)
    before = (iota((rows, rows), 0) < iota((rows, rows), 1)).astype(F32).astype(BF16)
    rank = jnp.sum(hot * nn(hot_b, before), axis=0, keepdims=True)
    line_k = jnp.sum(hot * target.astype(F32), axis=0, keepdims=True)
    slot = (line_k * cap + rank).astype(jnp.int32)
    tag_row = (ids[...] + 1).astype(F32)
    rank_hot = (iota((128, rows), 0) == rank.astype(jnp.int32)).astype(F32).astype(BF16)
    tag_slots = nt((hot * tag_row).astype(BF16), rank_hot)
    for k in range(n):
        send_tags[k] = jnp.broadcast_to(tag_slots[k : k + 1, :], (8, 128))

    pick = (iota((groups, rows), 0) == ids[...]).astype(F32).astype(BF16)
    ctf_hi, ctf_mid, ctf_lo = three(ctf[...])
    ctf_rows = tn(pick, ctf_hi) + tn(pick, ctf_mid) + tn(pick, ctf_lo)
    loads[4].wait()
    weighted[:, :half] = (img[:, :half].astype(F32) * ctf_rows).astype(BF16)
    weighted[:, half:] = (img[:, half:].astype(F32) * ctf_rows).astype(BF16)

    for b in range(batches):
        place = (iota((span, rows), 0) + b * span == slot).astype(F32).astype(BF16)
        send_lines[b * PER_BATCH : (b + 1) * PER_BATCH] = (
            nn(place, weighted[...]).astype(BF16).reshape(PER_BATCH, cap, width)
        )
    lines[0] = send_lines[0]
    tags[0] = send_tags[0]

    pl.semaphore_wait(barrier, len(partners) + odd)
    loads[3].wait()

    slot_ref = ref_all.at[core, pair, y_hi, odd]
    ag = copy(refs, slot_ref, s_ag.at[0], r_ag.at[odd], choose(across, near))
    ag.start()
    ag_2 = copy(refs, slot_ref, s_ag.at[1], r_ag.at[1], beyond)

    @pl.when(odd == 1)
    def _():
        ag_2.start()

    @pl.when(odd == 0)
    def _():
        ref_all[core, pair, y_hi, 0] = refs[...]

    sends = []

    def send_slots(k):
        line_copy = copy(send_lines.at[k], lines.at[k], s_line.at[k], r_line.at[k], to(k))
        tag_copy = copy(send_tags.at[k], tags.at[k], s_tag.at[k], r_tag.at[k], to(k))
        tag_copy.start()
        line_copy.start()
        return [tag_copy, line_copy]

    for k in reversed(range(1, n)):
        if OFFSETS[k][2] == 0:
            sends += send_slots(k)

    @pl.when(odd == 1)
    def _():
        copy(refs, ref_all.at[core, pair, y_hi, 0], s_ag.at[0], r_ag.at[0], across).wait_recv()
        ag_2.wait_send()

    copy(refs, ref_all.at[core, pair, y_hi, 1], s_ag.at[0], r_ag.at[1], across).wait_recv()
    mine = ref_all.at[core, pair, y_hi]
    ag_y = [copy(mine, mine, s_agy.at[d - 1], r_agy.at[d - 1], y_peer(d)) for d in range(1, N_YHI)]
    for c in ag_y:
        c.start()
    blocks = [ref_all.at[core, pair, (y_hi + N_YHI - d) % N_YHI] for d in range(N_YHI)]
    ag_x = [copy(p, p, s_agx.at[d], r_agx.at[d], x_peer) for d, p in enumerate(blocks)]
    ag_x[0].start()

    for k in reversed(range(1, n)):
        if OFFSETS[k][2]:
            sends += send_slots(k)

    k_loc = N_CORE * N_X * N_YHI * per
    ctf_sq = ctf[...] * ctf[...]
    ctf_sq4 = jnp.concatenate([ctf_sq] * (128 // groups), axis=0).astype(BF16)
    p_rows = k_loc // 4

    def set_quad(c, p):
        reference = ref_all[c, p].reshape(p_rows, width)
        re, im = reference[:, :half].astype(F32), reference[:, half:].astype(F32)
        power = (re * re + im * im).astype(BF16)
        hi, mid, lo = three(-0.5 * nt(power, ctf_sq4))
        lane = iota((p_rows, 128), 1)
        parts = jnp.where(lane < 2 * groups, mid.astype(F32), jnp.where(lane < 3 * groups, lo.astype(F32), 0.0))
        quad[c, p] = jnp.where(lane < groups, hi.astype(F32), parts).astype(BF16)

    for d in (1, 3, 2):
        ag_y[d - 1].wait_recv()
        ag_x[d].start()
    mine, theirs = ref_all.at[core, pair], ref_all.at[core, 1 - pair]
    ag_c = [copy(p, p, s_agc.at[i], r_agc.at[i], sibling) for i, p in enumerate((mine, theirs))]
    ag_c[0].start()
    set_quad(core, pair)
    ag_c[0].wait_recv()
    set_quad(1 - core, pair)
    for c in ag_x:
        c.wait_recv()
    ag_c[1].start()
    set_quad(core, 1 - pair)
    ag_c[1].wait_recv()
    set_quad(1 - core, 1 - pair)
    sends += [ag] + ag_y + ag_x + ag_c

    scale = width**-0.5
    spread = (iota((128, span), 0) == iota((128, span), 1) % cap).astype(F32).astype(BF16)
    mine_8 = (iota((PER_BATCH * 8, span), 0) == 8 * (iota((PER_BATCH * 8, span), 1) // cap)).astype(F32)
    tag_of = (iota((128, span), 0) % groups + 1).astype(F32)
    ev_sends = []
    for b in range(batches):
        for j in range(PER_BATCH):
            k = b * PER_BATCH + j
            if k:
                copy(send_tags.at[k], tags.at[k], s_tag.at[k], r_tag.at[k], to(k)).wait_recv()
                copy(send_lines.at[k], lines.at[k], s_line.at[k], r_line.at[k], to(k)).wait_recv()
        here = slice(b * span, (b + 1) * span)
        batch = lines[b * PER_BATCH : (b + 1) * PER_BATCH].reshape(span, width)
        tag8 = tags[b * PER_BATCH : (b + 1) * PER_BATCH].reshape(PER_BATCH * 8, 128).astype(BF16)
        tag = jnp.sum(nn(tag8, spread) * mine_8, axis=0, keepdims=True)
        pick = (tag_of == tag).astype(F32).astype(BF16)
        chosen[:, here] = pick
        score = nt(ref_all[...].reshape(k_loc, width), batch) + nn(quad[...].reshape(k_loc, 128), pick)
        score *= scale
        top = jnp.max(score, axis=0, keepdims=True)
        e = jnp.exp(score - top)
        total = jnp.sum(e, axis=0, keepdims=True)
        resp[:, here] = (e * (1.0 / total)).astype(BF16)
        send_ev[b] = top + jnp.log(total)
        for j in range(PER_BATCH):
            k = b * PER_BATCH + j
            if k:
                ev_copy = copy(send_ev.at[b], ev.at[k], s_ev.at[k], r_ev.at[k], back(k))
                ev_copy.start()
                ev_sends.append(ev_copy)
            else:
                ev[0] = send_ev[0]

    h_rows = k_loc // N_CORE
    x_rows = h_rows // 2
    own_lanes = iota((h_rows, 128), 1) // groups == (iota((h_rows, 128), 0) // 8) % (2 * per // 8)

    def sum_half(c):
        r = resp[pl.ds(pl.multiple_of(c * h_rows, h_rows), h_rows), :]
        acc[c] = nn(r, lines[...].reshape(n * cap, width))
        count = jnp.where(own_lanes, nt(r, chosen[...]), 0.0)
        return jnp.sum(count.reshape(2, N_YHI, 2 * per // 8, 8, 128), axis=2)

    rcore_out[...] = sum_half(1 - core)
    core_sends = [copy(rcore_out, rcore_in, s_rcc, r_rcc, sibling)]
    for i, xp in enumerate((1 - pair, pair)):
        at = pl.ds(pl.multiple_of(xp * x_rows, x_rows), x_rows)
        core_sends.append(copy(acc.at[1 - core, at], core_in.at[at], s_rsc.at[i], r_rsc.at[i], sibling))
    for c in core_sends:
        c.start()
    racc[...] = sum_half(core)

    core_sends[0].wait_recv()
    rx_out[...] = racc[...] + rcore_in[...]
    rc = copy(rx_out.at[1 - pair], rx_in, s_rcx, r_rcx, x_peer)
    rc.start()
    x_sends = []
    turns = (2, 1, 3, 0)
    core_sends[1].wait_recv()

    def rows_of(d, first=0):
        at = first + ((y_hi + d) % N_YHI) * 2 * per
        return pl.ds(pl.multiple_of(at, 2 * per), 2 * per)

    for i, d in enumerate(turns):
        at, far_at = rows_of(d), rows_of(d, (1 - pair) * x_rows)
        x_out[at] = (acc[core, far_at] + core_in[far_at]).astype(BF16)
        x_sends.append(copy(x_out.at[at], x_in.at[at], s_rsx.at[i], r_rsx.at[i], x_peer))
        x_sends[-1].start()
    core_sends[2].wait_recv()
    near_at = pl.ds(pl.multiple_of(pair * x_rows, x_rows), x_rows)
    own_rows[...] = acc[core, near_at] + core_in[near_at]

    rc.wait_recv()
    own_cnt = rx_out[pair] + rx_in[...]
    ry_out[...] = own_cnt
    y_sends = []
    for i, d in enumerate(turns[:-1]):
        x_sends[i].wait_recv()
        at = rows_of(d)
        y_out[d - 1] = (own_rows[at] + x_in[at].astype(F32)).astype(BF16)
        yc = copy(y_out.at[d - 1], y_in.at[d - 1], s_rsy.at[d - 1], r_rsy.at[d - 1], y_peer(d))
        rcy = copy(ry_out.at[(y_hi + d) % N_YHI], ry_in.at[d - 1], s_rcy.at[d - 1], r_rcy.at[d - 1], y_peer(d))
        rcy.start()
        yc.start()
        y_sends += [rcy, yc]
    x_sends[-1].wait_recv()
    x_sends.append(rc)

    for c in ev_sends:
        c.wait_recv()
    at_lane = line_k - PER_BATCH * jnp.floor(line_k * (1.0 / PER_BATCH))
    lane_hot = (iota((span, rows), 0) == (at_lane * cap + rank).astype(jnp.int32)).astype(F32).astype(BF16)
    e_hi, e_mid, e_lo = three(ev[:, 0, :])
    by_target = nn(e_hi, lane_hot) + nn(e_mid, lane_hot) + nn(e_lo, lane_hot)
    line_ev[...] = jnp.sum(hot * by_target, axis=0, keepdims=True)

    at = rows_of(0)
    part = own_rows[at] + x_in[at].astype(F32)
    for c in y_sends:
        c.wait_recv()
    count = ry_out[y_hi]
    for d in range(1, N_YHI):
        part += y_in[d - 1].astype(F32)
        count += ry_in[d - 1]
    fin_out[...] = part.reshape(2, per, width).astype(BF16)
    rfin_out[...] = count

    def fins(src, dst, i, dev):
        return (
            copy(rfin_out, rfin_in.at[dst], s_rfin.at[i], r_rfin.at[dst], dev),
            copy(fin_out.at[src], fin_in.at[dst], s_fin.at[i], r_fin.at[dst], dev),
        )

    fin = fins(1 - odd, odd, 0, choose(near, across))
    fin_2 = fins(1, 1, 1, beyond)
    for c in fin:
        c.start()

    @pl.when(odd == 1)
    def _():
        for c in fin_2:
            c.start()
        for c in fins(0, 0, 0, near):
            c.wait_recv()

    @pl.when(odd == 0)
    def _():
        fin_in[0] = fin_out[0]
        rfin_in[0] = rfin_out[...]

    for c in fins(0, 1, 0, near):
        c.wait_recv()
    final = fin_in[0].astype(F32) + fin_in[1].astype(F32)
    tile = rfin_in[0] + rfin_in[1]
    cnt = jnp.concatenate([tile] * (per // 8), axis=0)
    cnt = jnp.where(iota((per, 128), 1) // groups == iota((per, 128), 0) // 8 + odd * (per // 8), cnt, 0.0)
    c_hi, c_mid, c_lo = three(cnt)
    den = nn(c_hi, ctf_sq4) + nn(c_mid, ctf_sq4) + nn(c_lo, ctf_sq4) + 1.0
    out[:, :half] = final[:, :half] / den
    out[:, half:] = final[:, half:] / den

    @pl.when(odd == 1)
    def _():
        for c in fin_2:
            c.wait_send()

    for c in sends + ev_sends + core_sends + x_sends + y_sends + list(fin):
        c.wait_send()


def on_device(images, references, ctf_table, ctf_ids, owners):
    rows, width = images.shape
    per = references.shape[0]
    n = len(OFFSETS)
    cap = 3 * rows // n
    h_rows = N_X * N_YHI * per
    x_rows = h_rows // 2
    dma = pltpu.SemaphoreType.DMA
    vm = pltpu.VMEM
    scratch = [
        vm((rows, width), BF16), vm((per, width), BF16), vm(ctf_table.shape, F32),
        vm((1, rows), jnp.int32), vm((1, rows), jnp.int32),
        vm((rows, width), BF16), vm((n, cap, width), BF16), vm((n, cap, width), BF16),
        vm((n, 8, 128), F32), vm((n, 8, 128), F32),
        vm((n // PER_BATCH, 1, PER_BATCH * cap), F32), vm((n, 1, PER_BATCH * cap), F32),
        vm((N_CORE, 2, N_YHI, 2, per, width), BF16), vm((N_CORE * h_rows, n * cap), BF16), vm((128, n * cap), BF16),
        vm((N_CORE, 2, x_rows, 128), BF16), vm((N_CORE, h_rows, width), F32), vm((2, N_YHI, 8, 128), F32),
        vm((h_rows, width), F32), vm((2, N_YHI, 8, 128), F32), vm((2, N_YHI, 8, 128), F32),
        vm((x_rows, width), BF16), vm((x_rows, width), BF16), vm((2, N_YHI, 8, 128), F32), vm((N_YHI, 8, 128), F32),
        vm((x_rows, width), F32),
        vm((N_YHI - 1, 2 * per, width), BF16), vm((N_YHI - 1, 2 * per, width), BF16),
        vm((N_YHI, 8, 128), F32), vm((N_YHI - 1, 8, 128), F32),
        vm((2, per, width), BF16), vm((2, per, width), BF16), vm((8, 128), F32), vm((2, 8, 128), F32),
        dma((5,)),
        *[dma((n,))] * 6,
        *[dma((2,))] * 2, *[dma((N_YHI - 1,))] * 2, *[dma((N_YHI,))] * 2, *[dma((2,))] * 2,
        *[dma((2,))] * 2, *[dma] * 2, *[dma((N_YHI,))] * 2, *[dma] * 2, *[dma((N_YHI - 1,))] * 4,
        *[dma((2,))] * 4,
    ]
    new, ev = pl.pallas_call(
        kernel,
        out_shape=(jax.ShapeDtypeStruct((per, width), F32), jax.ShapeDtypeStruct((1, rows), F32)),
        in_specs=[pl.BlockSpec(memory_space=pltpu.HBM)] * 5,
        out_specs=[pl.BlockSpec(memory_space=pltpu.VMEM)] * 2,
        scratch_shapes=scratch,
        compiler_params=pltpu.CompilerParams(
            collective_id=0, has_side_effects=True, vmem_limit_bytes=62 * 2**20
        ),
    )(images, references, ctf_table, ctf_ids.reshape(1, rows), owners.reshape(1, rows))
    return new, ev.reshape(rows)


def solution(mesh):
    both = P(("slab", "group"))
    rows = P(("slab", "group"), None)
    return jax.shard_map(
        on_device, mesh=mesh, in_specs=(rows, rows, P(), both, both), out_specs=(rows, both), check_vma=False
    )
```

```python
import functools

import jax
import jax.numpy as jnp
from jax import lax
from jax.experimental import pallas as pl
from jax.experimental.pallas import tpu as pltpu
from jax.sharding import PartitionSpec as P

F32, BF16 = jnp.float32, jnp.bfloat16
MESH = pl.DeviceIdType.MESH
N_X, N_Y, N_Z = 4, 8, 8
N_YLO, N_YHI, N_CORE = 2, 4, 2
FAR = N_Z // 2
OFFSETS = tuple((dz, dx * (1 - 2 * dy), dy) for dz in (0, 1, -1, 2) for dy in (0, 1) for dx in (0, 1))
PER_BATCH = 8


def nt(a, b):
    return lax.dot_general(a, b, (((1,), (1,)), ((), ())), preferred_element_type=F32)


def tn(a, b):
    return lax.dot_general(a, b, (((0,), (0,)), ((), ())), preferred_element_type=F32)


def nn(a, b):
    return jnp.dot(a, b, preferred_element_type=F32)


def three(v):
    hi = v.astype(BF16)
    rest = v - hi.astype(F32)
    mid = rest.astype(BF16)
    return hi, mid, (rest - mid.astype(F32)).astype(BF16)


def iota(shape, dim):
    return lax.broadcasted_iota(jnp.int32, shape, dim)


def kernel(
    img_hbm, refs_hbm, ctf_hbm, ids_hbm, own_hbm,
    out, line_ev,
    img, refs, ctf, ids, own,
    weighted, send_lines, lines, send_tags, tags, send_ev, ev,
    ref_all, resp, chosen, quad, acc, racc,
    core_in, rcore_out, rcore_in, x_out, x_in, rx_out, rx_in, own_rows, y_out, y_in, ry_out, ry_in,
    fin_out, fin_in, rfin_out, rfin_in,
    ctf_sq4, spread, owner_row, tag_of, own_lanes, lane_hot, hot_lines,
    s_in,
    s_line, r_line, s_tag, r_tag, s_ev, r_ev,
    s_ag, r_ag, s_agy, r_agy, s_agx, r_agx, s_agc, r_agc,
    s_rsc, r_rsc, s_rcc, r_rcc, s_rsx, r_rsx, s_rcx, r_rcx, s_rsy, r_rsy, s_rcy, r_rcy,
    s_fin, r_fin, s_rfin, r_rfin,
):
    rows, width = img.shape
    per = refs.shape[0]
    half = width // 2
    groups = ctf.shape[0]
    n = len(OFFSETS)
    cap = 3 * rows // n
    batches = n // PER_BATCH
    span = PER_BATCH * cap
    slab, group = lax.axis_index("slab"), lax.axis_index("group")
    y_lo, z = lax.div(slab, N_Z), lax.rem(slab, N_Z)
    x, core = lax.div(group, N_YHI * N_CORE), lax.rem(group, N_CORE)
    y_hi = lax.rem(lax.div(group, N_CORE), N_YHI)
    y = N_YLO * y_hi + y_lo
    way = 1 - 2 * core
    odd, pair = lax.rem(x, 2), lax.div(x, 2)

    @functools.cache
    def z_to(step, turn=0):
        return lax.rem(z + way * step + N_Z + turn, N_Z)

    @functools.cache
    def x_to(step):
        return lax.rem(x + way * step + N_X, N_X)

    @functools.cache
    def y_to(step):
        to = lax.rem(y + way * step + N_Y, N_Y)
        return lax.rem(to, N_YLO), lax.div(to, N_YLO)

    @functools.cache
    def slab_row(dz, dy):
        return y_to(dy)[0] * N_Z + z_to(dz)

    @functools.cache
    def group_row(dx, dy):
        return (x_to(dx) * N_YHI + y_to(dy)[1]) * N_CORE + core

    def to(k):
        dz, dx, dy = OFFSETS[k]
        return slab_row(dz, dy), group_row(dx, dy)

    def back(k):
        dz, dx, dy = (-d for d in OFFSETS[k])
        return slab_row(dz, dy), group_row(dx, dy)

    def slab_of(k):
        dz, dx, dy = OFFSETS[k]
        return y_to(dy)[0] * N_Z + lax.rem(z_to(dz) + FAR * lax.rem(x_to(dx), 2), N_Z)

    @functools.cache
    def y_hi_to(d):
        return lax.rem(y_hi + d, N_YHI)

    def y_peer(d):
        return slab, (x * N_YHI + y_hi_to(d)) * N_CORE + core

    x_peer = slab, (lax.rem(x + 2, N_X) * N_YHI + y_hi) * N_CORE + core
    sibling = (slab, group + way)
    far_slab = y_lo * N_Z + z_to(0, FAR)
    near_group = ((x + 1 - 2 * odd) * N_YHI + y_hi) * N_CORE + core
    near, across, beyond = (slab, near_group), (far_slab, near_group), (far_slab, group)

    def choose(a, b):
        return tuple(odd * v + (1 - odd) * u for u, v in zip(a, b))

    def copy(src, dst, send, recv, device):
        return pltpu.make_async_remote_copy(
            src_ref=src, dst_ref=dst, send_sem=send, recv_sem=recv, device_id=device, device_id_type=MESH
        )

    loads = [
        pltpu.make_async_copy(a, b, s_in.at[i])
        for i, (a, b) in enumerate(((own_hbm, own), (ids_hbm, ids), (ctf_hbm, ctf), (refs_hbm, refs), (img_hbm, img)))
    ]
    for c in loads:
        c.start()

    barrier = pltpu.get_barrier_semaphore()
    partners = [back(k) for k in range(1, n)]
    partners += [y_peer(d) for d in range(1, N_YHI)] + [x_peer, sibling, near, across]
    for p in partners:
        pl.semaphore_signal(barrier, inc=1, device_id=p, device_id_type=MESH)

    @pl.when(odd == 1)
    def _():
        pl.semaphore_signal(barrier, inc=1, device_id=beyond, device_id_type=MESH)

    for c in loads[:3]:
        c.wait()

    target = iota((n, rows), 0)
    wanted = jnp.zeros((n, rows), jnp.int32)
    for k in range(n):
        wanted = jnp.where(target == k, slab_of(k), wanted)
    hot = (wanted == own[...]).astype(F32)
    hot_b = hot.astype(BF16)
    before = (iota((rows, rows), 0) < iota((rows, rows), 1)).astype(F32).astype(BF16)
    rank = jnp.sum(hot * nn(hot_b, before), axis=0, keepdims=True)
    line_k = jnp.sum(hot * target.astype(F32), axis=0, keepdims=True)
    slot = (line_k * cap + rank).astype(jnp.int32)
    tag_row = (ids[...] + 1).astype(F32)
    rank_hot = (iota((128, rows), 0) == rank.astype(jnp.int32)).astype(F32).astype(BF16)
    tag_slots = nt((hot * tag_row).astype(BF16), rank_hot)
    for k in range(n):
        send_tags[k] = jnp.broadcast_to(tag_slots[k : k + 1, :], (8, 128))

    pick = (iota((groups, rows), 0) == ids[...]).astype(F32).astype(BF16)
    ctf_hi, ctf_mid, ctf_lo = three(ctf[...])
    ctf_rows = tn(pick, ctf_hi) + tn(pick, ctf_mid) + tn(pick, ctf_lo)
    loads[4].wait()
    weighted[:, :half] = (img[:, :half].astype(F32) * ctf_rows).astype(BF16)
    weighted[:, half:] = (img[:, half:].astype(F32) * ctf_rows).astype(BF16)

    for b in range(batches):
        place = (iota((span, rows), 0) + b * span == slot).astype(F32).astype(BF16)
        send_lines[b * PER_BATCH : (b + 1) * PER_BATCH] = (
            nn(place, weighted[...]).astype(BF16).reshape(PER_BATCH, cap, width)
        )
    lines[0] = send_lines[0]
    tags[0] = send_tags[0]

    k_loc = N_CORE * N_X * N_YHI * per
    h_rows = k_loc // N_CORE
    x_rows = h_rows // 2
    ctf_sq4[...] = jnp.concatenate([ctf[...] * ctf[...]] * (128 // groups), axis=0).astype(BF16)
    spread[...] = (iota((128, span), 0) == iota((128, span), 1) % cap).astype(F32).astype(BF16)
    owner_row[...] = (iota((PER_BATCH * 8, span), 0) == 8 * (iota((PER_BATCH * 8, span), 1) // cap)).astype(F32)
    tag_of[...] = (iota((128, span), 0) % groups + 1).astype(F32)
    row_tile = (iota((h_rows, 128), 0) // 8) % (2 * per // 8)
    own_lanes[...] = (iota((h_rows, 128), 1) // groups == row_tile).astype(F32)
    at_lane = line_k - PER_BATCH * jnp.floor(line_k * (1.0 / PER_BATCH))
    lane_hot[...] = (iota((span, rows), 0) == (at_lane * cap + rank).astype(jnp.int32)).astype(F32).astype(BF16)
    hot_lines[...] = hot

    pl.semaphore_wait(barrier, len(partners) + odd)
    loads[3].wait()

    slot_ref = ref_all.at[core, pair, y_hi, odd]
    ag = copy(refs, slot_ref, s_ag.at[0], r_ag.at[odd], choose(across, near))
    ag.start()
    ag_2 = copy(refs, slot_ref, s_ag.at[1], r_ag.at[1], beyond)

    @pl.when(odd == 1)
    def _():
        ag_2.start()

    @pl.when(odd == 0)
    def _():
        ref_all[core, pair, y_hi, 0] = refs[...]

    sends = []

    def send_slots(k):
        line_copy = copy(send_lines.at[k], lines.at[k], s_line.at[k], r_line.at[k], to(k))
        tag_copy = copy(send_tags.at[k], tags.at[k], s_tag.at[k], r_tag.at[k], to(k))
        tag_copy.start()
        line_copy.start()
        return [tag_copy, line_copy]

    for k in range(1, n):
        if not (OFFSETS[k][2] or OFFSETS[k][1]):
            sends += send_slots(k)

    @pl.when(odd == 1)
    def _():
        copy(refs, ref_all.at[core, pair, y_hi, 0], s_ag.at[0], r_ag.at[0], across).wait_recv()
        ag_2.wait_send()

    copy(refs, ref_all.at[core, pair, y_hi, 1], s_ag.at[0], r_ag.at[1], across).wait_recv()
    mine = ref_all.at[core, pair, y_hi]
    ag_y = [copy(mine, mine, s_agy.at[d - 1], r_agy.at[d - 1], y_peer(d)) for d in range(1, N_YHI)]
    for c in ag_y:
        c.start()
    blocks = [ref_all.at[core, pair, y_hi_to(N_YHI - d)] for d in range(N_YHI)]
    ag_x = [copy(p, p, s_agx.at[d], r_agx.at[d], x_peer) for d, p in enumerate(blocks)]
    ag_x[0].start()

    for k in range(1, n):
        if OFFSETS[k][2] or OFFSETS[k][1]:
            sends += send_slots(k)

    p_rows = k_loc // 4

    def set_quad(c, p):
        reference = ref_all[c, p].reshape(p_rows, width)
        re, im = reference[:, :half].astype(F32), reference[:, half:].astype(F32)
        power = (re * re + im * im).astype(BF16)
        hi, mid, lo = three(-0.5 * nt(power, ctf_sq4[...]))
        lane = iota((p_rows, 128), 1)
        parts = jnp.where(lane < 2 * groups, mid.astype(F32), jnp.where(lane < 3 * groups, lo.astype(F32), 0.0))
        quad[c, p] = jnp.where(lane < groups, hi.astype(F32), parts).astype(BF16)

    for d in (1, 3, 2):
        ag_y[d - 1].wait_recv()
        ag_x[d].start()
    mine, theirs = ref_all.at[core, pair], ref_all.at[core, 1 - pair]
    ag_c = [copy(p, p, s_agc.at[i], r_agc.at[i], sibling) for i, p in enumerate((mine, theirs))]
    ag_c[0].start()
    set_quad(core, pair)
    ag_c[0].wait_recv()
    set_quad(1 - core, pair)
    for c in ag_x:
        c.wait_recv()
    ag_c[1].start()
    set_quad(core, 1 - pair)
    ag_c[1].wait_recv()
    set_quad(1 - core, 1 - pair)
    sends += [ag] + ag_y + ag_x + ag_c

    scale = width**-0.5
    ev_sends = []
    for b in range(batches):
        for j in range(PER_BATCH):
            k = b * PER_BATCH + j
            if k:
                copy(send_tags.at[k], tags.at[k], s_tag.at[k], r_tag.at[k], to(k)).wait_recv()
                copy(send_lines.at[k], lines.at[k], s_line.at[k], r_line.at[k], to(k)).wait_recv()
        here = slice(b * span, (b + 1) * span)
        batch = lines[b * PER_BATCH : (b + 1) * PER_BATCH].reshape(span, width)
        tag8 = tags[b * PER_BATCH : (b + 1) * PER_BATCH].reshape(PER_BATCH * 8, 128).astype(BF16)
        tag = jnp.sum(nn(tag8, spread[...]) * owner_row[...], axis=0, keepdims=True)
        pick = (tag_of[...] == tag).astype(F32).astype(BF16)
        chosen[:, here] = pick
        score = nt(ref_all[...].reshape(k_loc, width), batch) + nn(quad[...].reshape(k_loc, 128), pick)
        score *= scale
        top = jnp.max(score, axis=0, keepdims=True)
        e = jnp.exp(score - top)
        total = jnp.sum(e, axis=0, keepdims=True)
        resp[:, here] = (e * (1.0 / total)).astype(BF16)
        send_ev[b] = top + jnp.log(total)
        for j in range(PER_BATCH):
            k = b * PER_BATCH + j
            if k:
                ev_copy = copy(send_ev.at[b], ev.at[k], s_ev.at[k], r_ev.at[k], back(k))
                ev_copy.start()
                ev_sends.append(ev_copy)
            else:
                ev[0] = send_ev[0]

    def sum_half(c):
        r = resp[pl.ds(pl.multiple_of(c * h_rows, h_rows), h_rows), :]
        acc[c] = nn(r, lines[...].reshape(n * cap, width))
        count = nt(r, chosen[...]) * own_lanes[...]
        return jnp.sum(count.reshape(2, N_YHI, 2 * per // 8, 8, 128), axis=2)

    rcore_out[...] = sum_half(1 - core)
    core_sends = [copy(rcore_out, rcore_in, s_rcc, r_rcc, sibling)]
    for i, xp in enumerate((1 - pair, pair)):
        at = pl.ds(pl.multiple_of(xp * x_rows, x_rows), x_rows)
        core_sends.append(copy(acc.at[1 - core, at], core_in.at[at], s_rsc.at[i], r_rsc.at[i], sibling))
    for c in core_sends:
        c.start()
    racc[...] = sum_half(core)

    core_sends[0].wait_recv()
    rx_out[...] = racc[...] + rcore_in[...]
    rc = copy(rx_out.at[1 - pair], rx_in, s_rcx, r_rcx, x_peer)
    rc.start()
    x_sends = []
    turns = (2, 1, 3, 0)
    core_sends[1].wait_recv()

    def rows_of(d, first=0):
        at = first + y_hi_to(d) * 2 * per
        return pl.ds(pl.multiple_of(at, 2 * per), 2 * per)

    for i, d in enumerate(turns):
        at, far_at = rows_of(d), rows_of(d, (1 - pair) * x_rows)
        x_out[at] = (acc[core, far_at] + core_in[far_at]).astype(BF16)
        x_sends.append(copy(x_out.at[at], x_in.at[at], s_rsx.at[i], r_rsx.at[i], x_peer))
        x_sends[-1].start()
    core_sends[2].wait_recv()
    near_at = pl.ds(pl.multiple_of(pair * x_rows, x_rows), x_rows)
    own_rows[...] = acc[core, near_at] + core_in[near_at]

    rc.wait_recv()
    own_cnt = rx_out[pair] + rx_in[...]
    ry_out[...] = own_cnt
    y_sends = []
    for i, d in enumerate(turns[:-1]):
        x_sends[i].wait_recv()
        at = rows_of(d)
        y_out[d - 1] = (own_rows[at] + x_in[at].astype(F32)).astype(BF16)
        yc = copy(y_out.at[d - 1], y_in.at[d - 1], s_rsy.at[d - 1], r_rsy.at[d - 1], y_peer(d))
        rcy = copy(ry_out.at[y_hi_to(d)], ry_in.at[d - 1], s_rcy.at[d - 1], r_rcy.at[d - 1], y_peer(d))
        rcy.start()
        yc.start()
        y_sends += [rcy, yc]
    x_sends[-1].wait_recv()
    x_sends.append(rc)

    for c in ev_sends:
        c.wait_recv()
    e_hi, e_mid, e_lo = three(ev[:, 0, :])
    by_target = nn(e_hi, lane_hot[...]) + nn(e_mid, lane_hot[...]) + nn(e_lo, lane_hot[...])
    line_ev[...] = jnp.sum(hot_lines[...] * by_target, axis=0, keepdims=True)

    at = rows_of(0)
    part = own_rows[at] + x_in[at].astype(F32)
    for c in y_sends:
        c.wait_recv()
    count = ry_out[y_hi]
    for d in range(1, N_YHI):
        part += y_in[d - 1].astype(F32)
        count += ry_in[d - 1]
    fin_out[...] = part.reshape(2, per, width).astype(BF16)
    rfin_out[...] = count

    def fins(src, dst, i, dev):
        return (
            copy(rfin_out, rfin_in.at[dst], s_rfin.at[i], r_rfin.at[dst], dev),
            copy(fin_out.at[src], fin_in.at[dst], s_fin.at[i], r_fin.at[dst], dev),
        )

    fin = fins(1 - odd, odd, 0, choose(near, across))
    fin_2 = fins(1, 1, 1, beyond)
    for c in fin:
        c.start()

    @pl.when(odd == 1)
    def _():
        for c in fin_2:
            c.start()
        for c in fins(0, 0, 0, near):
            c.wait_recv()

    @pl.when(odd == 0)
    def _():
        fin_in[0] = fin_out[0]
        rfin_in[0] = rfin_out[...]

    for c in fins(0, 1, 0, near):
        c.wait_recv()
    final = fin_in[0].astype(F32) + fin_in[1].astype(F32)
    tile = rfin_in[0] + rfin_in[1]
    cnt = jnp.concatenate([tile] * (per // 8), axis=0)
    cnt = jnp.where(iota((per, 128), 1) // groups == iota((per, 128), 0) // 8 + odd * (per // 8), cnt, 0.0)
    c_hi, c_mid, c_lo = three(cnt)
    den = nn(c_hi, ctf_sq4[...]) + nn(c_mid, ctf_sq4[...]) + nn(c_lo, ctf_sq4[...]) + 1.0
    out[:, :half] = final[:, :half] / den
    out[:, half:] = final[:, half:] / den

    @pl.when(odd == 1)
    def _():
        for c in fin_2:
            c.wait_send()

    for c in sends + ev_sends + core_sends + x_sends + y_sends + list(fin):
        c.wait_send()


def on_device(images, references, ctf_table, ctf_ids, owners):
    rows, width = images.shape
    per = references.shape[0]
    n = len(OFFSETS)
    cap = 3 * rows // n
    h_rows = N_X * N_YHI * per
    x_rows = h_rows // 2
    dma = pltpu.SemaphoreType.DMA
    vm = pltpu.VMEM
    scratch = [
        vm((rows, width), BF16), vm((per, width), BF16), vm(ctf_table.shape, F32),
        vm((1, rows), jnp.int32), vm((1, rows), jnp.int32),
        vm((rows, width), BF16), vm((n, cap, width), BF16), vm((n, cap, width), BF16),
        vm((n, 8, 128), F32), vm((n, 8, 128), F32),
        vm((n // PER_BATCH, 1, PER_BATCH * cap), F32), vm((n, 1, PER_BATCH * cap), F32),
        vm((N_CORE, 2, N_YHI, 2, per, width), BF16), vm((N_CORE * h_rows, n * cap), BF16), vm((128, n * cap), BF16),
        vm((N_CORE, 2, x_rows, 128), BF16), vm((N_CORE, h_rows, width), F32), vm((2, N_YHI, 8, 128), F32),
        vm((h_rows, width), F32), vm((2, N_YHI, 8, 128), F32), vm((2, N_YHI, 8, 128), F32),
        vm((x_rows, width), BF16), vm((x_rows, width), BF16), vm((2, N_YHI, 8, 128), F32), vm((N_YHI, 8, 128), F32),
        vm((x_rows, width), F32),
        vm((N_YHI - 1, 2 * per, width), BF16), vm((N_YHI - 1, 2 * per, width), BF16),
        vm((N_YHI, 8, 128), F32), vm((N_YHI - 1, 8, 128), F32),
        vm((2, per, width), BF16), vm((2, per, width), BF16), vm((8, 128), F32), vm((2, 8, 128), F32),
        vm((128, width // 2), BF16), vm((128, PER_BATCH * cap), BF16), vm((PER_BATCH * 8, PER_BATCH * cap), F32),
        vm((128, PER_BATCH * cap), F32), vm((h_rows, 128), F32), vm((PER_BATCH * cap, rows), BF16), vm((n, rows), F32),
        dma((5,)),
        *[dma((n,))] * 6,
        *[dma((2,))] * 2, *[dma((N_YHI - 1,))] * 2, *[dma((N_YHI,))] * 2, *[dma((2,))] * 2,
        *[dma((2,))] * 2, *[dma] * 2, *[dma((N_YHI,))] * 2, *[dma] * 2, *[dma((N_YHI - 1,))] * 4,
        *[dma((2,))] * 4,
    ]
    new, ev = pl.pallas_call(
        kernel,
        out_shape=(jax.ShapeDtypeStruct((per, width), F32), jax.ShapeDtypeStruct((1, rows), F32)),
        in_specs=[pl.BlockSpec(memory_space=pltpu.HBM)] * 5,
        out_specs=[pl.BlockSpec(memory_space=pltpu.VMEM)] * 2,
        scratch_shapes=scratch,
        compiler_params=pltpu.CompilerParams(
            collective_id=0, has_side_effects=True, vmem_limit_bytes=62 * 2**20
        ),
    )(images, references, ctf_table, ctf_ids.reshape(1, rows), owners.reshape(1, rows))
    return new, ev.reshape(rows)


def solution(mesh):
    both = P(("slab", "group"))
    rows = P(("slab", "group"), None)
    return jax.shard_map(
        on_device, mesh=mesh, in_specs=(rows, rows, P(), both, both), out_specs=(rows, both), check_vma=False
    )
```

```python
import functools

import jax
import jax.numpy as jnp
from jax import lax
from jax.experimental import pallas as pl
from jax.experimental.pallas import tpu as pltpu
from jax.sharding import PartitionSpec as P

F32, BF16 = jnp.float32, jnp.bfloat16
MESH = pl.DeviceIdType.MESH
N_X, N_Y, N_Z = 4, 8, 8
N_YLO, N_YHI, N_CORE = 2, 4, 2
FAR = N_Z // 2
OFFSETS = tuple((dz, dx * (1 - 2 * dy), dy) for dz in (0, 1, -1, 2) for dy in (0, 1) for dx in (0, 1))
PER_BATCH = 8


def nt(a, b):
    return lax.dot_general(a, b, (((1,), (1,)), ((), ())), preferred_element_type=F32)


def tn(a, b):
    return lax.dot_general(a, b, (((0,), (0,)), ((), ())), preferred_element_type=F32)


def nn(a, b):
    return jnp.dot(a, b, preferred_element_type=F32)


def three(v):
    hi = v.astype(BF16)
    rest = v - hi.astype(F32)
    mid = rest.astype(BF16)
    return hi, mid, (rest - mid.astype(F32)).astype(BF16)


def iota(shape, dim):
    return lax.broadcasted_iota(jnp.int32, shape, dim)


def kernel(
    img_hbm, refs_hbm, ctf_hbm, ids_hbm, own_hbm,
    out, line_ev,
    img, refs, ctf, ids, own,
    weighted, send_lines, lines, send_tags, tags, send_ev, ev,
    ref_all, resp, chosen, quad, acc, racc,
    core_in, rcore_out, rcore_in, x_out, x_in, rx_out, rx_in, own_rows, y_out, y_in, ry_out, ry_in,
    fin_out, fin_in, rfin_out, rfin_in,
    ctf_sq4, spread, owner_row, tag_of, own_lanes, lane_hot, hot_lines,
    s_in,
    s_line, r_line, s_tag, r_tag, s_ev, r_ev,
    s_ag, r_ag, s_agy, r_agy, s_agx, r_agx, s_agc, r_agc,
    s_rsc, r_rsc, s_rcc, r_rcc, s_rsx, r_rsx, s_rcx, r_rcx, s_rsy, r_rsy, s_rcy, r_rcy,
    s_fin, r_fin, s_rfin, r_rfin,
):
    rows, width = img.shape
    per = refs.shape[0]
    half = width // 2
    groups = ctf.shape[0]
    n = len(OFFSETS)
    cap = 3 * rows // n
    batches = n // PER_BATCH
    span = PER_BATCH * cap
    slab, group = lax.axis_index("slab"), lax.axis_index("group")
    y_lo, z = lax.div(slab, N_Z), lax.rem(slab, N_Z)
    x, core = lax.div(group, N_YHI * N_CORE), lax.rem(group, N_CORE)
    y_hi = lax.rem(lax.div(group, N_CORE), N_YHI)
    y = N_YLO * y_hi + y_lo
    way = 1 - 2 * core
    odd, pair = lax.rem(x, 2), lax.div(x, 2)

    @functools.cache
    def z_to(step, turn=0):
        return lax.rem(z + way * step + N_Z + turn, N_Z)

    @functools.cache
    def x_to(step):
        return lax.rem(x + way * step + N_X, N_X)

    @functools.cache
    def y_to(step):
        to = lax.rem(y + way * step + N_Y, N_Y)
        return lax.rem(to, N_YLO), lax.div(to, N_YLO)

    @functools.cache
    def slab_row(dz, dy):
        return y_to(dy)[0] * N_Z + z_to(dz)

    @functools.cache
    def group_row(dx, dy):
        return (x_to(dx) * N_YHI + y_to(dy)[1]) * N_CORE + core

    def to(k):
        dz, dx, dy = OFFSETS[k]
        return slab_row(dz, dy), group_row(dx, dy)

    def back(k):
        dz, dx, dy = (-d for d in OFFSETS[k])
        return slab_row(dz, dy), group_row(dx, dy)

    def slab_of(k):
        dz, dx, dy = OFFSETS[k]
        return y_to(dy)[0] * N_Z + lax.rem(z_to(dz) + FAR * lax.rem(x_to(dx), 2), N_Z)

    @functools.cache
    def y_hi_to(d):
        return lax.rem(y_hi + d, N_YHI)

    def y_peer(d):
        return slab, (x * N_YHI + y_hi_to(d)) * N_CORE + core

    x_peer = slab, (lax.rem(x + 2, N_X) * N_YHI + y_hi) * N_CORE + core
    sibling = (slab, group + way)
    far_slab = y_lo * N_Z + z_to(0, FAR)
    near_group = ((x + 1 - 2 * odd) * N_YHI + y_hi) * N_CORE + core
    near, across, beyond = (slab, near_group), (far_slab, near_group), (far_slab, group)

    def choose(a, b):
        return tuple(odd * v + (1 - odd) * u for u, v in zip(a, b))

    def copy(src, dst, send, recv, device):
        return pltpu.make_async_remote_copy(
            src_ref=src, dst_ref=dst, send_sem=send, recv_sem=recv, device_id=device, device_id_type=MESH
        )

    loads = [
        pltpu.make_async_copy(a, b, s_in.at[i])
        for i, (a, b) in enumerate(((own_hbm, own), (ids_hbm, ids), (ctf_hbm, ctf), (refs_hbm, refs), (img_hbm, img)))
    ]
    for c in loads:
        c.start()

    barrier = pltpu.get_barrier_semaphore()
    partners = [back(k) for k in range(1, n)]
    partners += [y_peer(d) for d in range(1, N_YHI)] + [x_peer, sibling, near, across]
    for p in partners:
        pl.semaphore_signal(barrier, inc=1, device_id=p, device_id_type=MESH)

    @pl.when(odd == 1)
    def _():
        pl.semaphore_signal(barrier, inc=1, device_id=beyond, device_id_type=MESH)

    for c in loads[:3]:
        c.wait()

    target = iota((n, rows), 0)
    wanted = jnp.zeros((n, rows), jnp.int32)
    for k in range(n):
        wanted = jnp.where(target == k, slab_of(k), wanted)
    hot = (wanted == own[...]).astype(F32)
    hot_b = hot.astype(BF16)
    before = (iota((rows, rows), 0) < iota((rows, rows), 1)).astype(F32).astype(BF16)
    rank = jnp.sum(hot * nn(hot_b, before), axis=0, keepdims=True)
    line_k = jnp.sum(hot * target.astype(F32), axis=0, keepdims=True)
    slot = (line_k * cap + rank).astype(jnp.int32)
    tag_row = (ids[...] + 1).astype(F32)
    rank_hot = (iota((128, rows), 0) == rank.astype(jnp.int32)).astype(F32).astype(BF16)
    tag_slots = nt((hot * tag_row).astype(BF16), rank_hot)
    for k in range(n):
        send_tags[k] = jnp.broadcast_to(tag_slots[k : k + 1, :], (8, 128))

    pick = (iota((groups, rows), 0) == ids[...]).astype(F32).astype(BF16)
    ctf_hi, ctf_mid, ctf_lo = three(ctf[...])
    ctf_rows = tn(pick, ctf_hi) + tn(pick, ctf_mid) + tn(pick, ctf_lo)
    loads[4].wait()
    weighted[:, :half] = (img[:, :half].astype(F32) * ctf_rows).astype(BF16)
    weighted[:, half:] = (img[:, half:].astype(F32) * ctf_rows).astype(BF16)

    for b in range(batches):
        place = (iota((span, rows), 0) + b * span == slot).astype(F32).astype(BF16)
        send_lines[b * PER_BATCH : (b + 1) * PER_BATCH] = (
            nn(place, weighted[...]).astype(BF16).reshape(PER_BATCH, cap, width)
        )
    lines[0] = send_lines[0]
    tags[0] = send_tags[0]

    k_loc = N_CORE * N_X * N_YHI * per
    h_rows = k_loc // N_CORE
    x_rows = h_rows // 2
    ctf_sq4[...] = jnp.concatenate([ctf[...] * ctf[...]] * (128 // groups), axis=0).astype(BF16)
    spread[...] = (iota((128, span), 0) == iota((128, span), 1) % cap).astype(F32).astype(BF16)
    owner_row[...] = (iota((PER_BATCH * 8, span), 0) == 8 * (iota((PER_BATCH * 8, span), 1) // cap)).astype(F32)
    tag_of[...] = (iota((128, span), 0) % groups + 1).astype(F32)
    row_tile = (iota((h_rows, 128), 0) // 8) % (2 * per // 8)
    own_lanes[...] = (iota((h_rows, 128), 1) // groups == row_tile).astype(F32)
    at_lane = line_k - PER_BATCH * jnp.floor(line_k * (1.0 / PER_BATCH))
    lane_hot[...] = (iota((span, rows), 0) == (at_lane * cap + rank).astype(jnp.int32)).astype(F32).astype(BF16)
    hot_lines[...] = hot

    pl.semaphore_wait(barrier, len(partners) + odd)
    loads[3].wait()

    slot_ref = ref_all.at[core, pair, y_hi, odd]
    ag = copy(refs, slot_ref, s_ag.at[0], r_ag.at[odd], choose(across, near))
    ag.start()
    ag_2 = copy(refs, slot_ref, s_ag.at[1], r_ag.at[1], beyond)

    @pl.when(odd == 1)
    def _():
        ag_2.start()

    @pl.when(odd == 0)
    def _():
        ref_all[core, pair, y_hi, 0] = refs[...]

    sends = []

    def send_slots(k):
        line_copy = copy(send_lines.at[k], lines.at[k], s_line.at[k], r_line.at[k], to(k))
        tag_copy = copy(send_tags.at[k], tags.at[k], s_tag.at[k], r_tag.at[k], to(k))
        tag_copy.start()
        line_copy.start()
        return [tag_copy, line_copy]

    for k in range(1, n):
        if not (OFFSETS[k][2] or OFFSETS[k][1]):
            sends += send_slots(k)

    @pl.when(odd == 1)
    def _():
        copy(refs, ref_all.at[core, pair, y_hi, 0], s_ag.at[0], r_ag.at[0], across).wait_recv()
        ag_2.wait_send()

    copy(refs, ref_all.at[core, pair, y_hi, 1], s_ag.at[0], r_ag.at[1], across).wait_recv()
    mine = ref_all.at[core, pair, y_hi]
    ag_y = [copy(mine, mine, s_agy.at[d - 1], r_agy.at[d - 1], y_peer(d)) for d in range(1, N_YHI)]
    for c in ag_y:
        c.start()
    blocks = [ref_all.at[core, pair, y_hi_to(N_YHI - d)] for d in range(N_YHI)]
    ag_x = [copy(p, p, s_agx.at[d], r_agx.at[d], x_peer) for d, p in enumerate(blocks)]
    ag_x[0].start()

    for k in range(1, n):
        if OFFSETS[k][2] or OFFSETS[k][1]:
            sends += send_slots(k)

    p_rows = k_loc // 4

    def set_quad(c, p):
        reference = ref_all[c, p].reshape(p_rows, width)
        re, im = reference[:, :half].astype(F32), reference[:, half:].astype(F32)
        power = (re * re + im * im).astype(BF16)
        hi, mid, lo = three(-0.5 * nt(power, ctf_sq4[...]))
        lane = iota((p_rows, 128), 1)
        parts = jnp.where(lane < 2 * groups, mid.astype(F32), jnp.where(lane < 3 * groups, lo.astype(F32), 0.0))
        quad[c, p] = jnp.where(lane < groups, hi.astype(F32), parts).astype(BF16)

    for d in (1, 3, 2):
        ag_y[d - 1].wait_recv()
        ag_x[d].start()
    mine, theirs = ref_all.at[core, pair], ref_all.at[core, 1 - pair]
    ag_c = [copy(p, p, s_agc.at[i], r_agc.at[i], sibling) for i, p in enumerate((mine, theirs))]
    ag_c[0].start()
    set_quad(core, pair)
    ag_c[0].wait_recv()
    set_quad(1 - core, pair)
    for c in ag_x:
        c.wait_recv()
    ag_c[1].start()
    set_quad(core, 1 - pair)
    ag_c[1].wait_recv()
    set_quad(1 - core, 1 - pair)
    sends += [ag] + ag_y + ag_x + ag_c

    scale = width**-0.5
    ev_sends = []
    for b in range(batches):
        for j in range(PER_BATCH):
            k = b * PER_BATCH + j
            if k:
                copy(send_tags.at[k], tags.at[k], s_tag.at[k], r_tag.at[k], to(k)).wait_recv()
                copy(send_lines.at[k], lines.at[k], s_line.at[k], r_line.at[k], to(k)).wait_recv()
        here = slice(b * span, (b + 1) * span)
        batch = lines[b * PER_BATCH : (b + 1) * PER_BATCH].reshape(span, width)
        tag8 = tags[b * PER_BATCH : (b + 1) * PER_BATCH].reshape(PER_BATCH * 8, 128).astype(BF16)
        tag = jnp.sum(nn(tag8, spread[...]) * owner_row[...], axis=0, keepdims=True)
        pick = (tag_of[...] == tag).astype(F32).astype(BF16)
        chosen[:, here] = pick
        score = nt(ref_all[...].reshape(k_loc, width), batch) + nn(quad[...].reshape(k_loc, 128), pick)
        score *= scale
        top = jnp.max(score, axis=0, keepdims=True)
        e = jnp.exp(score - top)
        total = jnp.sum(e, axis=0, keepdims=True)
        resp[:, here] = (e * (1.0 / total)).astype(BF16)
        send_ev[b] = top + jnp.log(total)
        for j in range(PER_BATCH):
            k = b * PER_BATCH + j
            if k:
                ev_copy = copy(send_ev.at[b], ev.at[k], s_ev.at[k], r_ev.at[k], back(k))
                ev_copy.start()
                ev_sends.append(ev_copy)
            else:
                ev[0] = send_ev[0]

    def sum_half(c):
        r = resp[pl.ds(pl.multiple_of(c * h_rows, h_rows), h_rows), :]
        acc[c] = nn(r, lines[...].reshape(n * cap, width))
        count = nt(r, chosen[...]) * own_lanes[...]
        return jnp.sum(count.reshape(2, N_YHI, 2 * per // 8, 8, 128), axis=2)

    rcore_out[...] = sum_half(1 - core)
    core_sends = [copy(rcore_out, rcore_in, s_rcc, r_rcc, sibling)]
    for i, xp in enumerate((1 - pair, pair)):
        at = pl.ds(pl.multiple_of(xp * x_rows, x_rows), x_rows)
        core_sends.append(copy(acc.at[1 - core, at], core_in.at[at], s_rsc.at[i], r_rsc.at[i], sibling))
    for c in core_sends:
        c.start()
    racc[...] = sum_half(core)

    core_sends[0].wait_recv()
    rx_out[...] = racc[...] + rcore_in[...]
    rc = copy(rx_out.at[1 - pair], rx_in, s_rcx, r_rcx, x_peer)
    rc.start()
    x_sends = []
    turns = (2, 1, 3, 0)
    core_sends[1].wait_recv()

    def rows_of(d, first=0):
        at = first + y_hi_to(d) * 2 * per
        return pl.ds(pl.multiple_of(at, 2 * per), 2 * per)

    for i, d in enumerate(turns):
        at, far_at = rows_of(d), rows_of(d, (1 - pair) * x_rows)
        x_out[at] = (acc[core, far_at] + core_in[far_at]).astype(BF16)
        x_sends.append(copy(x_out.at[at], x_in.at[at], s_rsx.at[i], r_rsx.at[i], x_peer))
        x_sends[-1].start()
    core_sends[2].wait_recv()
    near_at = pl.ds(pl.multiple_of(pair * x_rows, x_rows), x_rows)
    own_rows[...] = acc[core, near_at] + core_in[near_at]

    rc.wait_recv()
    own_cnt = rx_out[pair] + rx_in[...]
    ry_out[...] = own_cnt
    halves = 1 - odd, odd

    def half_of(d, h):
        return pl.ds(pl.multiple_of(y_hi_to(d) * 2 * per + halves[h] * per, per), per)

    count_sends = []
    for d in turns[:-1]:
        count_sends.append(
            copy(ry_out.at[y_hi_to(d)], ry_in.at[d - 1], s_rcy.at[d - 1], r_rcy.at[d - 1], y_peer(d))
        )
        count_sends[-1].start()
    y_sends = [[], []]
    for h in range(2):
        for i, d in enumerate(turns[:-1]):
            if h == 0:
                x_sends[i].wait_recv()
            at = half_of(d, h)
            y_out[h, d - 1] = (own_rows[at] + x_in[at].astype(F32)).astype(BF16)
            y_sends[h].append(
                copy(y_out.at[h, d - 1], y_in.at[h, d - 1], s_rsy.at[h, d - 1], r_rsy.at[h, d - 1], y_peer(d))
            )
            y_sends[h][-1].start()
    x_sends[-1].wait_recv()
    x_sends.append(rc)

    for c in ev_sends:
        c.wait_recv()
    e_hi, e_mid, e_lo = three(ev[:, 0, :])
    by_target = nn(e_hi, lane_hot[...]) + nn(e_mid, lane_hot[...]) + nn(e_lo, lane_hot[...])
    line_ev[...] = jnp.sum(hot_lines[...] * by_target, axis=0, keepdims=True)

    count = ry_out[y_hi]
    for c in count_sends:
        c.wait_recv()
    for d in range(1, N_YHI):
        count += ry_in[d - 1]
    rfin_out[...] = count

    def finish(h):
        part = own_rows[half_of(0, h)] + x_in[half_of(0, h)].astype(F32)
        for c in y_sends[h]:
            c.wait_recv()
        for d in range(1, N_YHI):
            part += y_in[h, d - 1].astype(F32)
        fin_out[halves[h]] = part.astype(BF16)

    def fins(src, dst, i, dev):
        return (
            copy(rfin_out, rfin_in.at[dst], s_rfin.at[i], r_rfin.at[dst], dev),
            copy(fin_out.at[src], fin_in.at[dst], s_fin.at[i], r_fin.at[dst], dev),
        )

    fin = fins(1 - odd, odd, 0, choose(near, across))
    fin_2 = fins(1, 1, 1, beyond)
    finish(0)
    for c in fin:
        c.start()
    finish(1)

    @pl.when(odd == 1)
    def _():
        for c in fin_2:
            c.start()
        for c in fins(0, 0, 0, near):
            c.wait_recv()

    @pl.when(odd == 0)
    def _():
        fin_in[0] = fin_out[0]
        rfin_in[0] = rfin_out[...]

    for c in fins(0, 1, 0, near):
        c.wait_recv()
    final = fin_in[0].astype(F32) + fin_in[1].astype(F32)
    tile = rfin_in[0] + rfin_in[1]
    cnt = jnp.concatenate([tile] * (per // 8), axis=0)
    cnt = jnp.where(iota((per, 128), 1) // groups == iota((per, 128), 0) // 8 + odd * (per // 8), cnt, 0.0)
    c_hi, c_mid, c_lo = three(cnt)
    den = nn(c_hi, ctf_sq4[...]) + nn(c_mid, ctf_sq4[...]) + nn(c_lo, ctf_sq4[...]) + 1.0
    out[:, :half] = final[:, :half] / den
    out[:, half:] = final[:, half:] / den

    @pl.when(odd == 1)
    def _():
        for c in fin_2:
            c.wait_send()

    for c in sends + ev_sends + core_sends + x_sends + count_sends + y_sends[0] + y_sends[1] + list(fin):
        c.wait_send()


def on_device(images, references, ctf_table, ctf_ids, owners):
    rows, width = images.shape
    per = references.shape[0]
    n = len(OFFSETS)
    cap = 3 * rows // n
    h_rows = N_X * N_YHI * per
    x_rows = h_rows // 2
    dma = pltpu.SemaphoreType.DMA
    vm = pltpu.VMEM
    scratch = [
        vm((rows, width), BF16), vm((per, width), BF16), vm(ctf_table.shape, F32),
        vm((1, rows), jnp.int32), vm((1, rows), jnp.int32),
        vm((rows, width), BF16), vm((n, cap, width), BF16), vm((n, cap, width), BF16),
        vm((n, 8, 128), F32), vm((n, 8, 128), F32),
        vm((n // PER_BATCH, 1, PER_BATCH * cap), F32), vm((n, 1, PER_BATCH * cap), F32),
        vm((N_CORE, 2, N_YHI, 2, per, width), BF16), vm((N_CORE * h_rows, n * cap), BF16), vm((128, n * cap), BF16),
        vm((N_CORE, 2, x_rows, 128), BF16), vm((N_CORE, h_rows, width), F32), vm((2, N_YHI, 8, 128), F32),
        vm((h_rows, width), F32), vm((2, N_YHI, 8, 128), F32), vm((2, N_YHI, 8, 128), F32),
        vm((x_rows, width), BF16), vm((x_rows, width), BF16), vm((2, N_YHI, 8, 128), F32), vm((N_YHI, 8, 128), F32),
        vm((x_rows, width), F32),
        vm((2, N_YHI - 1, per, width), BF16), vm((2, N_YHI - 1, per, width), BF16),
        vm((N_YHI, 8, 128), F32), vm((N_YHI - 1, 8, 128), F32),
        vm((2, per, width), BF16), vm((2, per, width), BF16), vm((8, 128), F32), vm((2, 8, 128), F32),
        vm((128, width // 2), BF16), vm((128, PER_BATCH * cap), BF16), vm((PER_BATCH * 8, PER_BATCH * cap), F32),
        vm((128, PER_BATCH * cap), F32), vm((h_rows, 128), F32), vm((PER_BATCH * cap, rows), BF16), vm((n, rows), F32),
        dma((5,)),
        *[dma((n,))] * 6,
        *[dma((2,))] * 2, *[dma((N_YHI - 1,))] * 2, *[dma((N_YHI,))] * 2, *[dma((2,))] * 2,
        *[dma((2,))] * 2, *[dma] * 2, *[dma((N_YHI,))] * 2, *[dma] * 2, *[dma((2, N_YHI - 1))] * 2, *[dma((N_YHI - 1,))] * 2,
        *[dma((2,))] * 4,
    ]
    new, ev = pl.pallas_call(
        kernel,
        out_shape=(jax.ShapeDtypeStruct((per, width), F32), jax.ShapeDtypeStruct((1, rows), F32)),
        in_specs=[pl.BlockSpec(memory_space=pltpu.HBM)] * 5,
        out_specs=[pl.BlockSpec(memory_space=pltpu.VMEM)] * 2,
        scratch_shapes=scratch,
        compiler_params=pltpu.CompilerParams(
            collective_id=0, has_side_effects=True, vmem_limit_bytes=62 * 2**20
        ),
    )(images, references, ctf_table, ctf_ids.reshape(1, rows), owners.reshape(1, rows))
    return new, ev.reshape(rows)


def solution(mesh):
    both = P(("slab", "group"))
    rows = P(("slab", "group"), None)
    return jax.shard_map(
        on_device, mesh=mesh, in_specs=(rows, rows, P(), both, both), out_specs=(rows, both), check_vma=False
    )
```

```python
import functools

import jax
import jax.numpy as jnp
from jax import lax
from jax.experimental import pallas as pl
from jax.experimental.pallas import tpu as pltpu
from jax.sharding import PartitionSpec as P

F32, BF16 = jnp.float32, jnp.bfloat16
MESH = pl.DeviceIdType.MESH
N_X, N_Y, N_Z = 4, 8, 8
N_YLO, N_YHI, N_CORE = 2, 4, 2
FAR = N_Z // 2
OFFSETS = tuple((dz, dx * (1 - 2 * dy), dy) for dz in (0, 1, -1, 2) for dy in (0, 1) for dx in (0, 1))
PER_BATCH = 8


def nt(a, b):
    return lax.dot_general(a, b, (((1,), (1,)), ((), ())), preferred_element_type=F32)


def tn(a, b):
    return lax.dot_general(a, b, (((0,), (0,)), ((), ())), preferred_element_type=F32)


def nn(a, b):
    return jnp.dot(a, b, preferred_element_type=F32)


def three(v):
    hi = v.astype(BF16)
    rest = v - hi.astype(F32)
    mid = rest.astype(BF16)
    return hi, mid, (rest - mid.astype(F32)).astype(BF16)


def iota(shape, dim):
    return lax.broadcasted_iota(jnp.int32, shape, dim)


def kernel(
    img_hbm, refs_hbm, ctf_hbm, ids_hbm, own_hbm,
    out, line_ev,
    img, refs, ctf, ids, own,
    weighted, send_lines, lines, send_tags, tags, send_ev, ev,
    ref_all, resp, chosen, quad, acc, racc,
    core_in, rcore_out, rcore_in, x_out, x_in, rx_out, rx_in, own_rows, y_out, y_in, ry_out, ry_in,
    fin_out, fin_in, rfin_out, rfin_in,
    ctf_sq4, spread, owner_row, tag_of, own_lanes, lane_hot, hot_lines,
    s_in,
    s_line, r_line, s_tag, r_tag, s_ev, r_ev,
    s_ag, r_ag, s_agy, r_agy, s_agx, r_agx, s_agc, r_agc,
    s_rsc, r_rsc, s_rcc, r_rcc, s_rsx, r_rsx, s_rcx, r_rcx, s_rsy, r_rsy, s_rcy, r_rcy,
    s_fin, r_fin, s_rfin, r_rfin,
):
    rows, width = img.shape
    per = refs.shape[0]
    half = width // 2
    groups = ctf.shape[0]
    n = len(OFFSETS)
    cap = 3 * rows // n
    batches = n // PER_BATCH
    span = PER_BATCH * cap
    slab, group = lax.axis_index("slab"), lax.axis_index("group")
    y_lo, z = lax.div(slab, N_Z), lax.rem(slab, N_Z)
    x, core = lax.div(group, N_YHI * N_CORE), lax.rem(group, N_CORE)
    y_hi = lax.rem(lax.div(group, N_CORE), N_YHI)
    y = N_YLO * y_hi + y_lo
    way = 1 - 2 * core
    odd, pair = lax.rem(x, 2), lax.div(x, 2)

    @functools.cache
    def z_to(step, turn=0):
        return lax.rem(z + way * step + N_Z + turn, N_Z)

    @functools.cache
    def x_to(step):
        return lax.rem(x + way * step + N_X, N_X)

    @functools.cache
    def y_to(step):
        to = lax.rem(y + way * step + N_Y, N_Y)
        return lax.rem(to, N_YLO), lax.div(to, N_YLO)

    @functools.cache
    def slab_row(dz, dy):
        return y_to(dy)[0] * N_Z + z_to(dz)

    @functools.cache
    def group_row(dx, dy):
        return (x_to(dx) * N_YHI + y_to(dy)[1]) * N_CORE + core

    def to(k):
        dz, dx, dy = OFFSETS[k]
        return slab_row(dz, dy), group_row(dx, dy)

    def back(k):
        dz, dx, dy = (-d for d in OFFSETS[k])
        return slab_row(dz, dy), group_row(dx, dy)

    def slab_of(k):
        dz, dx, dy = OFFSETS[k]
        return y_to(dy)[0] * N_Z + lax.rem(z_to(dz) + FAR * lax.rem(x_to(dx), 2), N_Z)

    @functools.cache
    def y_hi_to(d):
        return lax.rem(y_hi + d, N_YHI)

    def y_peer(d):
        return slab, (x * N_YHI + y_hi_to(d)) * N_CORE + core

    x_peer = slab, (lax.rem(x + 2, N_X) * N_YHI + y_hi) * N_CORE + core
    sibling = (slab, group + way)
    far_slab = y_lo * N_Z + z_to(0, FAR)
    near_group = ((x + 1 - 2 * odd) * N_YHI + y_hi) * N_CORE + core
    near, across, beyond = (slab, near_group), (far_slab, near_group), (far_slab, group)

    def choose(a, b):
        return tuple(odd * v + (1 - odd) * u for u, v in zip(a, b))

    def copy(src, dst, send, recv, device):
        return pltpu.make_async_remote_copy(
            src_ref=src, dst_ref=dst, send_sem=send, recv_sem=recv, device_id=device, device_id_type=MESH
        )

    loads = [
        pltpu.make_async_copy(a, b, s_in.at[i])
        for i, (a, b) in enumerate(((own_hbm, own), (ids_hbm, ids), (ctf_hbm, ctf), (refs_hbm, refs), (img_hbm, img)))
    ]
    for c in loads:
        c.start()

    barrier = pltpu.get_barrier_semaphore()
    partners = [back(k) for k in range(1, n)]
    partners += [y_peer(d) for d in range(1, N_YHI)] + [x_peer, sibling, near, across]
    for p in partners:
        pl.semaphore_signal(barrier, inc=1, device_id=p, device_id_type=MESH)

    @pl.when(odd == 1)
    def _():
        pl.semaphore_signal(barrier, inc=1, device_id=beyond, device_id_type=MESH)

    for c in loads[:3]:
        c.wait()

    target = iota((n, rows), 0)
    wanted = jnp.zeros((n, rows), jnp.int32)
    for k in range(n):
        wanted = jnp.where(target == k, slab_of(k), wanted)
    hot = (wanted == own[...]).astype(F32)
    hot_b = hot.astype(BF16)
    before = (iota((rows, rows), 0) < iota((rows, rows), 1)).astype(F32).astype(BF16)
    rank = jnp.sum(hot * nn(hot_b, before), axis=0, keepdims=True)
    line_k = jnp.sum(hot * target.astype(F32), axis=0, keepdims=True)
    slot = (line_k * cap + rank).astype(jnp.int32)
    tag_row = (ids[...] + 1).astype(F32)
    rank_hot = (iota((128, rows), 0) == rank.astype(jnp.int32)).astype(F32).astype(BF16)
    tag_slots = nt((hot * tag_row).astype(BF16), rank_hot)
    for k in range(n):
        send_tags[k] = tag_slots[k : k + 1, :]

    pick = (iota((groups, rows), 0) == ids[...]).astype(F32).astype(BF16)
    ctf_hi, ctf_mid, ctf_lo = three(ctf[...])
    ctf_rows = tn(pick, ctf_hi) + tn(pick, ctf_mid) + tn(pick, ctf_lo)
    loads[4].wait()
    weighted[:, :half] = (img[:, :half].astype(F32) * ctf_rows).astype(BF16)
    weighted[:, half:] = (img[:, half:].astype(F32) * ctf_rows).astype(BF16)

    for b in range(batches):
        place = (iota((span, rows), 0) + b * span == slot).astype(F32).astype(BF16)
        send_lines[b * PER_BATCH : (b + 1) * PER_BATCH] = (
            nn(place, weighted[...]).astype(BF16).reshape(PER_BATCH, cap, width)
        )
    lines[0] = send_lines[0]
    tags[0] = send_tags[0]

    k_loc = N_CORE * N_X * N_YHI * per
    h_rows = k_loc // N_CORE
    x_rows = h_rows // 2
    ctf_sq4[...] = jnp.concatenate([ctf[...] * ctf[...]] * (128 // groups), axis=0).astype(BF16)
    spread[...] = (iota((128, span), 0) == iota((128, span), 1) % cap).astype(F32).astype(BF16)
    owner_row[...] = (iota((PER_BATCH, span), 0) == iota((PER_BATCH, span), 1) // cap).astype(F32)
    tag_of[...] = (iota((128, span), 0) % groups + 1).astype(F32)
    row_tile = (iota((h_rows, 128), 0) // 8) % (2 * per // 8)
    own_lanes[...] = (iota((h_rows, 128), 1) // groups == row_tile).astype(F32)
    at_lane = line_k - PER_BATCH * jnp.floor(line_k * (1.0 / PER_BATCH))
    lane_hot[...] = (iota((span, rows), 0) == (at_lane * cap + rank).astype(jnp.int32)).astype(F32).astype(BF16)
    hot_lines[...] = hot

    pl.semaphore_wait(barrier, len(partners) + odd)
    loads[3].wait()

    slot_ref = ref_all.at[core, pair, y_hi, odd]
    ag = copy(refs, slot_ref, s_ag.at[0], r_ag.at[odd], choose(across, near))
    ag.start()
    ag_2 = copy(refs, slot_ref, s_ag.at[1], r_ag.at[1], beyond)

    @pl.when(odd == 1)
    def _():
        ag_2.start()

    @pl.when(odd == 0)
    def _():
        ref_all[core, pair, y_hi, 0] = refs[...]

    sends = []

    def send_slots(k):
        line_copy = copy(send_lines.at[k], lines.at[k], s_line.at[k], r_line.at[k], to(k))
        tag_copy = copy(send_tags.at[k], tags.at[k], s_tag.at[k], r_tag.at[k], to(k))
        tag_copy.start()
        line_copy.start()
        return [tag_copy, line_copy]

    for k in range(1, n):
        if not (OFFSETS[k][2] or OFFSETS[k][1]):
            sends += send_slots(k)

    @pl.when(odd == 1)
    def _():
        copy(refs, ref_all.at[core, pair, y_hi, 0], s_ag.at[0], r_ag.at[0], across).wait_recv()
        ag_2.wait_send()

    copy(refs, ref_all.at[core, pair, y_hi, 1], s_ag.at[0], r_ag.at[1], across).wait_recv()
    mine = ref_all.at[core, pair, y_hi]
    ag_y = [copy(mine, mine, s_agy.at[d - 1], r_agy.at[d - 1], y_peer(d)) for d in range(1, N_YHI)]
    for c in ag_y:
        c.start()
    blocks = [ref_all.at[core, pair, y_hi_to(N_YHI - d)] for d in range(N_YHI)]
    ag_x = [copy(p, p, s_agx.at[d], r_agx.at[d], x_peer) for d, p in enumerate(blocks)]
    ag_x[0].start()

    for k in range(1, n):
        if OFFSETS[k][2] or OFFSETS[k][1]:
            sends += send_slots(k)

    p_rows = k_loc // 4

    def set_quad(c, p):
        reference = ref_all[c, p].reshape(p_rows, width)
        re, im = reference[:, :half].astype(F32), reference[:, half:].astype(F32)
        power = (re * re + im * im).astype(BF16)
        hi, mid, lo = three(-0.5 * nt(power, ctf_sq4[...]))
        lane = iota((p_rows, 128), 1)
        parts = jnp.where(lane < 2 * groups, mid.astype(F32), jnp.where(lane < 3 * groups, lo.astype(F32), 0.0))
        quad[c, p] = jnp.where(lane < groups, hi.astype(F32), parts).astype(BF16)

    for d in (1, 3, 2):
        ag_y[d - 1].wait_recv()
        ag_x[d].start()
    mine, theirs = ref_all.at[core, pair], ref_all.at[core, 1 - pair]
    ag_c = [copy(p, p, s_agc.at[i], r_agc.at[i], sibling) for i, p in enumerate((mine, theirs))]
    ag_c[0].start()
    set_quad(core, pair)
    ag_c[0].wait_recv()
    set_quad(1 - core, pair)
    for c in ag_x:
        c.wait_recv()
    ag_c[1].start()
    set_quad(core, 1 - pair)
    ag_c[1].wait_recv()
    set_quad(1 - core, 1 - pair)
    sends += [ag] + ag_y + ag_x + ag_c

    scale = width**-0.5
    ev_sends = []
    for b in range(batches):
        for j in range(PER_BATCH):
            k = b * PER_BATCH + j
            if k:
                copy(send_tags.at[k], tags.at[k], s_tag.at[k], r_tag.at[k], to(k)).wait_recv()
                copy(send_lines.at[k], lines.at[k], s_line.at[k], r_line.at[k], to(k)).wait_recv()
        here = slice(b * span, (b + 1) * span)
        batch = lines[b * PER_BATCH : (b + 1) * PER_BATCH].reshape(span, width)
        tag8 = tags[b * PER_BATCH : (b + 1) * PER_BATCH, 0, :].astype(BF16)
        tag = jnp.sum(nn(tag8, spread[...]) * owner_row[...], axis=0, keepdims=True)
        pick = (tag_of[...] == tag).astype(F32).astype(BF16)
        chosen[:, here] = pick
        score = nt(ref_all[...].reshape(k_loc, width), batch) + nn(quad[...].reshape(k_loc, 128), pick)
        score *= scale
        top = jnp.max(score, axis=0, keepdims=True)
        e = jnp.exp(score - top)
        total = jnp.sum(e, axis=0, keepdims=True)
        resp[:, here] = (e * (1.0 / total)).astype(BF16)
        send_ev[b] = top + jnp.log(total)
        for j in range(PER_BATCH):
            k = b * PER_BATCH + j
            if k:
                ev_copy = copy(send_ev.at[b], ev.at[k], s_ev.at[k], r_ev.at[k], back(k))
                ev_copy.start()
                ev_sends.append(ev_copy)
            else:
                ev[0] = send_ev[0]

    def sum_half(c):
        r = resp[pl.ds(pl.multiple_of(c * h_rows, h_rows), h_rows), :]
        acc[c] = nn(r, lines[...].reshape(n * cap, width))
        count = nt(r, chosen[...]) * own_lanes[...]
        return jnp.sum(count.reshape(2, N_YHI, 2 * per // 8, 8, 128), axis=2)

    rcore_out[...] = sum_half(1 - core)
    core_sends = [copy(rcore_out, rcore_in, s_rcc, r_rcc, sibling)]
    for i, xp in enumerate((1 - pair, pair)):
        at = pl.ds(pl.multiple_of(xp * x_rows, x_rows), x_rows)
        core_sends.append(copy(acc.at[1 - core, at], core_in.at[at], s_rsc.at[i], r_rsc.at[i], sibling))
    for c in core_sends:
        c.start()
    racc[...] = sum_half(core)

    core_sends[0].wait_recv()
    rx_out[...] = racc[...] + rcore_in[...]
    rc = copy(rx_out.at[1 - pair], rx_in, s_rcx, r_rcx, x_peer)
    rc.start()
    x_sends = []
    turns = (2, 1, 3, 0)
    core_sends[1].wait_recv()

    def rows_of(d, first=0):
        at = first + y_hi_to(d) * 2 * per
        return pl.ds(pl.multiple_of(at, 2 * per), 2 * per)

    for i, d in enumerate(turns):
        at, far_at = rows_of(d), rows_of(d, (1 - pair) * x_rows)
        x_out[at] = (acc[core, far_at] + core_in[far_at]).astype(BF16)
        x_sends.append(copy(x_out.at[at], x_in.at[at], s_rsx.at[i], r_rsx.at[i], x_peer))
        x_sends[-1].start()
    core_sends[2].wait_recv()
    near_at = pl.ds(pl.multiple_of(pair * x_rows, x_rows), x_rows)
    own_rows[...] = acc[core, near_at] + core_in[near_at]

    rc.wait_recv()
    own_cnt = rx_out[pair] + rx_in[...]
    ry_out[...] = own_cnt
    halves = 1 - odd, odd

    def half_of(d, h):
        return pl.ds(pl.multiple_of(y_hi_to(d) * 2 * per + halves[h] * per, per), per)

    count_sends = []
    for d in turns[:-1]:
        count_sends.append(
            copy(ry_out.at[y_hi_to(d)], ry_in.at[d - 1], s_rcy.at[d - 1], r_rcy.at[d - 1], y_peer(d))
        )
        count_sends[-1].start()
    y_sends = [[], []]
    for h in range(2):
        for i, d in enumerate(turns[:-1]):
            if h == 0:
                x_sends[i].wait_recv()
            at = half_of(d, h)
            y_out[h, d - 1] = (own_rows[at] + x_in[at].astype(F32)).astype(BF16)
            y_sends[h].append(
                copy(y_out.at[h, d - 1], y_in.at[h, d - 1], s_rsy.at[h, d - 1], r_rsy.at[h, d - 1], y_peer(d))
            )
            y_sends[h][-1].start()
    x_sends[-1].wait_recv()
    x_sends.append(rc)

    for c in ev_sends:
        c.wait_recv()
    e_hi, e_mid, e_lo = three(ev[:, 0, :])
    by_target = nn(e_hi, lane_hot[...]) + nn(e_mid, lane_hot[...]) + nn(e_lo, lane_hot[...])
    line_ev[...] = jnp.sum(hot_lines[...] * by_target, axis=0, keepdims=True)

    count = ry_out[y_hi]
    for c in count_sends:
        c.wait_recv()
    for d in range(1, N_YHI):
        count += ry_in[d - 1]
    rfin_out[...] = count

    def finish(h):
        part = own_rows[half_of(0, h)] + x_in[half_of(0, h)].astype(F32)
        for c in y_sends[h]:
            c.wait_recv()
        for d in range(1, N_YHI):
            part += y_in[h, d - 1].astype(F32)
        fin_out[halves[h]] = part.astype(BF16)

    def fins(src, dst, i, dev):
        return (
            copy(rfin_out, rfin_in.at[dst], s_rfin.at[i], r_rfin.at[dst], dev),
            copy(fin_out.at[src], fin_in.at[dst], s_fin.at[i], r_fin.at[dst], dev),
        )

    fin = fins(1 - odd, odd, 0, choose(near, across))
    fin_2 = fins(1, 1, 1, beyond)
    finish(0)
    for c in fin:
        c.start()
    finish(1)

    @pl.when(odd == 1)
    def _():
        for c in fin_2:
            c.start()
        for c in fins(0, 0, 0, near):
            c.wait_recv()

    @pl.when(odd == 0)
    def _():
        fin_in[0] = fin_out[0]
        rfin_in[0] = rfin_out[...]

    for c in fins(0, 1, 0, near):
        c.wait_recv()
    final = fin_in[0].astype(F32) + fin_in[1].astype(F32)
    tile = rfin_in[0] + rfin_in[1]
    cnt = jnp.concatenate([tile] * (per // 8), axis=0)
    cnt = jnp.where(iota((per, 128), 1) // groups == iota((per, 128), 0) // 8 + odd * (per // 8), cnt, 0.0)
    c_hi, c_mid, c_lo = three(cnt)
    den = nn(c_hi, ctf_sq4[...]) + nn(c_mid, ctf_sq4[...]) + nn(c_lo, ctf_sq4[...]) + 1.0
    out[:, :half] = final[:, :half] / den
    out[:, half:] = final[:, half:] / den

    @pl.when(odd == 1)
    def _():
        for c in fin_2:
            c.wait_send()

    for c in sends + ev_sends + core_sends + x_sends + count_sends + y_sends[0] + y_sends[1] + list(fin):
        c.wait_send()


def on_device(images, references, ctf_table, ctf_ids, owners):
    rows, width = images.shape
    per = references.shape[0]
    n = len(OFFSETS)
    cap = 3 * rows // n
    h_rows = N_X * N_YHI * per
    x_rows = h_rows // 2
    dma = pltpu.SemaphoreType.DMA
    vm = pltpu.VMEM
    scratch = [
        vm((rows, width), BF16), vm((per, width), BF16), vm(ctf_table.shape, F32),
        vm((1, rows), jnp.int32), vm((1, rows), jnp.int32),
        vm((rows, width), BF16), vm((n, cap, width), BF16), vm((n, cap, width), BF16),
        vm((n, 1, 128), F32), vm((n, 1, 128), F32),
        vm((n // PER_BATCH, 1, PER_BATCH * cap), F32), vm((n, 1, PER_BATCH * cap), F32),
        vm((N_CORE, 2, N_YHI, 2, per, width), BF16), vm((N_CORE * h_rows, n * cap), BF16), vm((128, n * cap), BF16),
        vm((N_CORE, 2, x_rows, 128), BF16), vm((N_CORE, h_rows, width), F32), vm((2, N_YHI, 8, 128), F32),
        vm((h_rows, width), F32), vm((2, N_YHI, 8, 128), F32), vm((2, N_YHI, 8, 128), F32),
        vm((x_rows, width), BF16), vm((x_rows, width), BF16), vm((2, N_YHI, 8, 128), F32), vm((N_YHI, 8, 128), F32),
        vm((x_rows, width), F32),
        vm((2, N_YHI - 1, per, width), BF16), vm((2, N_YHI - 1, per, width), BF16),
        vm((N_YHI, 8, 128), F32), vm((N_YHI - 1, 8, 128), F32),
        vm((2, per, width), BF16), vm((2, per, width), BF16), vm((8, 128), F32), vm((2, 8, 128), F32),
        vm((128, width // 2), BF16), vm((128, PER_BATCH * cap), BF16), vm((PER_BATCH, PER_BATCH * cap), F32),
        vm((128, PER_BATCH * cap), F32), vm((h_rows, 128), F32), vm((PER_BATCH * cap, rows), BF16), vm((n, rows), F32),
        dma((5,)),
        *[dma((n,))] * 6,
        *[dma((2,))] * 2, *[dma((N_YHI - 1,))] * 2, *[dma((N_YHI,))] * 2, *[dma((2,))] * 2,
        *[dma((2,))] * 2, *[dma] * 2, *[dma((N_YHI,))] * 2, *[dma] * 2, *[dma((2, N_YHI - 1))] * 2, *[dma((N_YHI - 1,))] * 2,
        *[dma((2,))] * 4,
    ]
    new, ev = pl.pallas_call(
        kernel,
        out_shape=(jax.ShapeDtypeStruct((per, width), F32), jax.ShapeDtypeStruct((1, rows), F32)),
        in_specs=[pl.BlockSpec(memory_space=pltpu.HBM)] * 5,
        out_specs=[pl.BlockSpec(memory_space=pltpu.VMEM)] * 2,
        scratch_shapes=scratch,
        compiler_params=pltpu.CompilerParams(
            collective_id=0, has_side_effects=True, vmem_limit_bytes=62 * 2**20
        ),
    )(images, references, ctf_table, ctf_ids.reshape(1, rows), owners.reshape(1, rows))
    return new, ev.reshape(rows)


def solution(mesh):
    both = P(("slab", "group"))
    rows = P(("slab", "group"), None)
    return jax.shard_map(
        on_device, mesh=mesh, in_specs=(rows, rows, P(), both, both), out_specs=(rows, both), check_vma=False
    )
```
